512 devices in a mesh: dp: 32 (over x, z_lo), mp: 16 (over y, z_hi, core).
Axes of the slice: x: 4, y: 4, z: 16 (z_hi: 2, z_lo: 8; z = z_hi * 8 + z_lo), core: 2. Of those that a mesh axis runs over, the one named last changes fastest.
Arguments:
- tokens: bfloat16 [8192, 4096], P('dp', 'mp'), may hold values from -1200 to 1200
- norm_gain: bfloat16 [4096], P('mp'), may hold values from 0.099609375 to 1.8984375
- w_inner: bfloat16 [4096, 12288], P('dp', 'mp'), may hold values from -0.09375 to 0.09375
- w_outer: bfloat16 [12288, 4096], P('mp', 'dp'), may hold values from -0.109375 to 0.109375
Outputs:
- mlp_out: bfloat16 [8192, 4096], P('dp', 'mp')
The draws below stay inside these ranges and needn't reach their ends.
All inputs are finite; a program needn't handle non-finite values.
Results may differ from the reference program's by a relative error of at most 0.017.
Values may be sent and summed in bfloat16 or wider, within the bound.
No kernel may reach another device: no remote copies, remote signals or barrier semaphores. Data moves between devices by JAX's collectives and lax.ppermute only.
A program may use at most 64 MiB of HBM per device.

```python
import jax
import jax.numpy as jnp
from jax import lax

D = 4096
FF = 12288
TOKENS = 8192
FF_DEV = 768


def draw_tokens(key, part):
    key = jax.random.fold_in(key, 11)
    key_base, key_cols, key_rows = jax.random.split(key, 3)
    rising = jnp.exp(jnp.log(3.0) * jnp.arange(D, dtype=jnp.float32) / max(D - 1, 1))
    col_scale = jnp.exp(jax.random.uniform(key_cols, (D,), jnp.float32) * jnp.log(10.0)) * rising
    row_scale = jnp.exp(jax.random.uniform(key_rows, (TOKENS, 1), jnp.float32) * jnp.log(10.0))
    base = jnp.clip(jax.random.normal(key_base, (TOKENS, D), jnp.float32), -4.0, 4.0)
    return (base * row_scale * col_scale[None, :]).astype(jnp.bfloat16)


def with_spikes(entries, rng, source, target, shards_of, factor):
    owner, partner = [(jnp.arange(entries.shape[axis_at]) // (entries.shape[axis_at] // shards_of)).reshape([-1 if axis == axis_at else 1 for axis in range(entries.ndim)]) for axis_at in (source, target)]
    chosen = jax.random.permutation(rng, shards_of)[partner]
    strong = (owner == chosen) | (owner == (partner + shards_of // 2) % shards_of)
    return jnp.where(strong, factor * entries, entries)


def shard_levels(own_key, dims, cuts, low, top_value):
    def one(dim, blocks):
        heights = jax.random.uniform(jax.random.fold_in(jax.random.fold_in(own_key, 6), dim), (blocks,), jnp.float32, low / len(cuts), top_value / len(cuts))
        return jnp.repeat(jnp.exp(heights), dims[dim] // blocks).reshape((-1,) + (1,) * (len(dims) - dim - 1))

    factor_of = one(*cuts[0])
    for cut in cuts[1:]:
        factor_of = factor_of * one(*cut)
    return factor_of


def noise(key, extent, width, bound, cuts=(), held_as=jnp.bfloat16):
    result = jax.random.normal(key, extent, jnp.float32) * width
    if len(cuts) > 0:
        result = shard_levels(key, extent, cuts, -0.22, 0.18) * result
    return jnp.clip(result, min=-bound, max=bound).astype(held_as)


def bell_draw_with(key, extent, scale, reach, cuts, heavy, kind=jnp.bfloat16):
    array = scale * jax.random.normal(key, extent, jnp.float32)
    if cuts:
        array = array * shard_levels(key, extent, cuts, -0.22, 0.18)
    return jnp.clip(with_spikes(array, jax.random.fold_in(key, 3), *heavy), -reach, reach).astype(kind)


def setup_inputs(seed: int = 0) -> dict:
    key_list = jax.random.split(jax.random.key(seed), 5)
    return {
        "tokens": draw_tokens(jax.random.fold_in(key_list[4], 71), 0),
        "norm_gain": jnp.clip(1.0 + 0.18 * jax.random.normal(key_list[1], (D,), jnp.float32), 0.099609375, 1.8984375).astype(jnp.bfloat16),
        "w_inner": noise(key_list[2], (D, FF), D ** -0.5, 0.09375, ((0, 32), (1, 16))),
        "w_outer": bell_draw_with(key_list[3], (FF, D), FF ** -0.5, 0.109375, ((0, 16), (1, 32)), (0, 1, 32, 2.75)),
    }


epsilon = 1e-06

def gelu_exact(values):
    return 0.5 * values * (1.0 + lax.erf(values * 0.7071067811865476))

def reference(tokens, norm_gain, w_inner, w_outer):
    values = tokens.astype(jnp.float32)
    center = lax.optimization_barrier(jnp.mean(values, axis=1, keepdims=True))
    spread = lax.optimization_barrier(jnp.mean(jnp.square(values - center), axis=1, keepdims=True))
    normed = ((values - center) * lax.rsqrt(spread + epsilon) * norm_gain.astype(jnp.float32)).astype(jnp.bfloat16)

    def add_block(index, total):
        begin = (index * FF_DEV).astype(jnp.int32)
        columns = lax.dynamic_slice_in_dim(w_inner, begin, FF_DEV, 1)
        weight_rows = lax.dynamic_slice_in_dim(w_outer, begin, FF_DEV, 0)
        hidden_pre = jnp.dot(normed, columns, preferred_element_type=jnp.float32)
        activated = gelu_exact(hidden_pre).astype(jnp.bfloat16)
        block_term = jnp.dot(activated, weight_rows, preferred_element_type=jnp.float32).astype(jnp.bfloat16)
        return total + block_term.astype(jnp.float32)
    summed = lax.fori_loop(0, FF // FF_DEV, add_block, jnp.zeros((TOKENS, D), jnp.float32))
    return summed.astype(jnp.bfloat16)
```

```python
import jax
import jax.numpy as jnp
import numpy as np
from jax import lax
from jax.sharding import Mesh, PartitionSpec as P

epsilon = 1e-06
AXES = ("x", "zt", "zq", "y", "zh", "c")
SIZES = (4, 2, 4, 4, 2, 2)
SIZE = dict(zip(AXES, SIZES))


def gelu_exact(values):
    return 0.5 * values * (1.0 + lax.erf(values * 0.7071067811865476))


def xor_send(value, axes, k):
    count = int(np.prod([SIZE[a] for a in axes]))
    return lax.ppermute(value, axes, [(i, i ^ k) for i in range(count)])


def put(buffer, piece, indices):
    full = list(indices) + [0] * (buffer.ndim - len(indices))
    return lax.dynamic_update_slice(
        buffer, piece.reshape((1,) * len(indices) + piece.shape), full
    )


def pick(array, indices):
    for index in indices:
        array = lax.dynamic_index_in_dim(array, index, 0, keepdims=False)
    return array


def swap_halves(pieces, zt, c):
    straight = lax.ppermute(
        pick(pieces, [zt]), ("zt", "c"), [(2 * a + b, 2 * b + a) for a in (0, 1) for b in (0, 1)]
    )
    crossed = lax.ppermute(
        pick(pieces, [1 - zt]), ("zt", "c"), [(2 * a + b, 2 * b + 1 - a) for a in (0, 1) for b in (0, 1)]
    )
    first = c == 0
    return jnp.stack([jnp.where(first, straight, crossed), jnp.where(first, crossed, straight)])


def gather_axis(value, axis):
    me = lax.axis_index(axis)
    buffer = jnp.zeros((SIZE[axis],) + value.shape, value.dtype)
    buffer = put(buffer, value, [me])
    for k in range(1, SIZE[axis]):
        buffer = put(buffer, xor_send(value, (axis,), k), [me ^ k])
    return buffer


def per_device(tokens, norm_gain, w_inner, w_outer):
    zt, zh, y, c = (lax.axis_index(a) for a in ("zt", "zh", "y", "c"))
    rows, cols = tokens.shape
    d_dev, f_dev = w_inner.shape
    half = f_dev // 2
    with jax.named_scope("inner_weights"):
        inner = jnp.stack([w_inner[:, :half], w_inner[:, half:]])
        inner = swap_halves(inner, zt, c)
        inner = jnp.swapaxes(gather_axis(inner, "zq"), 0, 1)
        inner = gather_axis(inner, "x").reshape(-1, half)
    with jax.named_scope("outer_weights"):
        outer = w_outer.reshape(2, half, d_dev)
        outer = swap_halves(outer, zt, c)
        outer = jnp.swapaxes(gather_axis(outer, "zq"), 0, 1)
        outer = gather_axis(outer, "x").reshape(-1, half, d_dev)
    with jax.named_scope("tokens"):
        both = jnp.concatenate([tokens, jnp.broadcast_to(norm_gain[None], (16, cols))], axis=0)
        buffer = jnp.zeros((2, 2) + both.shape, both.dtype)
        buffer = put(buffer, both, [zt, zh])
        for k in (1, 2, 3):
            got = xor_send(both, ("zt", "zh"), k)
            buffer = put(buffer, got, [zt ^ (k >> 1), zh ^ (k & 1)])
        buffer = gather_axis(buffer, "y")
        buffer = gather_axis(buffer, "c")
        buffer = buffer.transpose(2, 4, 1, 3, 0, 5)
        full_gain = buffer[0, rows].reshape(-1)
        values = buffer[:, :rows].reshape(2 * rows, -1).astype(jnp.float32)
    center = jnp.mean(values, axis=1, keepdims=True)
    spread = jnp.mean(jnp.square(values - center), axis=1, keepdims=True)
    normed = (
        (values - center) * lax.rsqrt(spread + epsilon) * full_gain.astype(jnp.float32)
    ).astype(jnp.bfloat16)
    hidden_pre = jnp.dot(normed, inner, preferred_element_type=jnp.float32)
    activated = gelu_exact(hidden_pre).astype(jnp.bfloat16)
    partial = jnp.einsum("tf,zfd->tzd", activated, outer, preferred_element_type=jnp.float32)
    with jax.named_scope("outputs"):
        partial = partial.reshape(2, rows, SIZE["y"], 2, 2, cols).transpose(4, 2, 0, 3, 1, 5)
        mine = pick(partial, [c]) + xor_send(
            pick(partial, [1 - c]).astype(jnp.bfloat16), ("c",), 1
        ).astype(jnp.float32)
        sent = mine.astype(jnp.bfloat16)
        total = pick(mine, [y])
        for k in (1, 2, 3):
            total = total + xor_send(pick(sent, [y ^ k]), ("y",), k).astype(jnp.float32)
        sent = total.astype(jnp.bfloat16)
        result = pick(total, [zt, zh])
        for k in (1, 2, 3):
            result = result + xor_send(
                pick(sent, [zt ^ (k >> 1), zh ^ (k & 1)]), ("zt", "zh"), k
            ).astype(jnp.float32)
    return result.astype(jnp.bfloat16)


def solution(mesh):
    fine = Mesh(np.asarray(mesh.devices).reshape(SIZES), AXES)
    dp, mp = ("x", "zt", "zq"), ("y", "zh", "c")
    in_specs = (P(dp, mp), P(mp), P(dp, mp), P(mp, dp))
    return jax.shard_map(
        per_device, mesh=fine, in_specs=in_specs, out_specs=P(dp, mp), check_vma=False
    )
```

```python
import jax
import jax.numpy as jnp
import numpy as np
from jax import lax
from jax.experimental import pallas as pl
from jax.experimental.pallas import tpu as pltpu
from jax.sharding import Mesh, PartitionSpec as P

epsilon = 1e-06
AXES = ("x", "zt", "zq", "y", "zh", "c")
SIZES = (4, 2, 4, 4, 2, 2)
SIZE = dict(zip(AXES, SIZES))
GAIN_ROWS = 16


def gelu_exact(values):
    return 0.5 * values * (1.0 + lax.erf(values * 0.7071067811865476))


def send(value, axes, k):
    count = int(np.prod([SIZE[a] for a in axes]))
    return lax.ppermute(value, axes, [(i, i ^ k) for i in range(count)])


def after(value, *others):
    return lax.optimization_barrier((value, *others))[0]


def swap_halves(first, second):
    both = [(a, b) for a in (0, 1) for b in (0, 1)]
    straight = lax.ppermute(first, ("zt", "c"), [(2 * a + b, 2 * b + a) for a, b in both])
    crossed = lax.ppermute(second, ("zt", "c"), [(2 * a + b, 2 * b + 1 - a) for a, b in both])
    return straight, crossed


def coordinates():
    return {a: lax.axis_index(a) for a in AXES}


def hidden_kernel(place, mine, other, w0, w1, w2, w3, act):
    x, zq, y, zh, c = (place[i] for i in range(5))
    cores = (mine, other)
    rows = act.shape[1]
    width = mine.shape[3]
    count = 2 * mine.shape[0] * 2 * width
    for a in range(2):
        blocks = [(ref, i, 2 * a + j) for ref in cores for i in range(4) for j in range(2)]
        total = jnp.zeros((rows, width), jnp.float32)
        for ref, i, j in blocks:
            total += ref[i, j, :rows, :].astype(jnp.float32)
        center = jnp.sum(total, axis=1, keepdims=True) * (1.0 / count)
        total = jnp.zeros((rows, width), jnp.float32)
        for ref, i, j in blocks:
            total += jnp.square(ref[i, j, :rows, :].astype(jnp.float32) - center)
        spread = jnp.sum(total, axis=1, keepdims=True) * (1.0 / count)
        scale = lax.rsqrt(spread + epsilon)
        acc = jnp.zeros((rows, act.shape[2]), jnp.float32)
        for k, weights in enumerate((w0, w1, w2, w3)):
            i = x ^ k ^ y
            for s in range(2):
                j = 2 * a + (zh ^ c ^ s)
                for ck, ref in enumerate(cores):
                    first = 2 * (c ^ ck)
                    block = jnp.concatenate(
                        [weights[first ^ zq, s], weights[(first + 1) ^ zq, s]], axis=0
                    )
                    gain = ref[i, j, rows : rows + GAIN_ROWS, :].astype(jnp.float32)[0:1]
                    values = ref[i, j, :rows, :].astype(jnp.float32)
                    normed = ((values - center) * scale * gain).astype(jnp.bfloat16)
                    acc += jnp.dot(normed, block, preferred_element_type=jnp.float32)
        act[a] = gelu_exact(acc).astype(act.dtype)


def out_kernel(place, act, w0, w1, w2, w3, mine, other):
    x, zq, y, zh, c = (place[i] for i in range(5))
    for ck, ref in ((1, other), (0, mine)):
        first = 2 * (c ^ ck)
        for k, weights in enumerate((w0, w1, w2, w3)):
            i = x ^ k ^ y
            for s in range(2):
                block = jnp.concatenate(
                    [weights[first ^ zq, s], weights[(first + 1) ^ zq, s]], axis=1
                )
                for a in range(2):
                    ref[i, 2 * a + (zh ^ c ^ s)] = jnp.dot(
                        act[a], block, preferred_element_type=jnp.float32
                    ).astype(ref.dtype)


def call(kernel, out_shape, flops, *operands):
    vmem = pl.BlockSpec(memory_space=pltpu.VMEM)
    size = sum(o.size * o.dtype.itemsize for o in operands)
    return pl.pallas_call(
        kernel,
        out_shape=out_shape,
        in_specs=[pl.BlockSpec(memory_space=pltpu.SMEM)] + [vmem] * (len(operands) - 1),
        out_specs=jax.tree.map(lambda _: vmem, out_shape),
        compiler_params=pltpu.CompilerParams(vmem_limit_bytes=40 * 1024 * 1024),
        cost_estimate=pl.CostEstimate(flops=flops, bytes_accessed=size, transcendentals=0),
    )(*operands)


def per_device(tokens, norm_gain, w_inner, w_outer):
    at = coordinates()
    zt = at["zt"]
    rows, cols = tokens.shape
    d_dev, f_dev = w_inner.shape
    half = f_dev // 2
    place = jnp.stack([at[a] for a in ("x", "zq", "y", "zh", "c")]).astype(jnp.int32)

    def weight_half(which, axis, array):
        return lax.dynamic_slice_in_dim(array, which * half, half, axis)

    swapped = swap_halves(weight_half(zt, 1, w_inner), weight_half(1 - zt, 1, w_inner))
    inner = jnp.stack(swapped)
    inner = jnp.stack([inner] + [send(inner, ("zq",), k) for k in (1, 2, 3)])

    both = jnp.concatenate([tokens, jnp.broadcast_to(norm_gain[None], (GAIN_ROWS, cols))], axis=0)
    both = after(both, *swapped)
    both = jnp.stack([both] + [send(both, ("zt", "zh"), k) for k in (1, 2, 3)])

    inner_all = [inner] + [send(inner, ("x",), k) for k in (1, 2, 3)]

    outer = jnp.stack(
        swap_halves(*(weight_half(h, 0, after(w_outer, inner)) for h in (zt, 1 - zt)))
    )
    outer = jnp.stack([outer] + [send(outer, ("zq",), k) for k in (1, 2, 3)])

    both = after(both, inner)
    both = jnp.stack([both] + [send(both, ("y",), k) for k in (1, 2, 3)])
    other = send(both, ("c",), 1)
    outer_all = [outer] + [send(after(outer, inner_all[k]), ("x",), k) for k in (1, 2, 3)]

    flops = 2 * 2 * rows * half * 16 * cols
    act = call(
        hidden_kernel,
        jax.ShapeDtypeStruct((2, rows, half), jnp.bfloat16),
        flops, place, both, other, *inner_all,
    )
    shape = jax.ShapeDtypeStruct((4, 4, rows, cols), jnp.bfloat16)
    mine, other = call(out_kernel, (shape, shape), flops, place, act, *outer_all)

    total = mine.astype(jnp.float32) + send(other, ("c",), 1).astype(jnp.float32)
    sent = total.astype(jnp.bfloat16)
    total = total[0] + sum(send(sent[k], ("y",), k).astype(jnp.float32) for k in (1, 2, 3))
    sent = total.astype(jnp.bfloat16)
    total = total[0] + sum(send(sent[k], ("zt", "zh"), k).astype(jnp.float32) for k in (1, 2, 3))
    return total.astype(jnp.bfloat16)


def solution(mesh):
    fine = Mesh(np.asarray(mesh.devices).reshape(SIZES), AXES)
    dp, mp = ("x", "zt", "zq"), ("y", "zh", "c")
    in_specs = (P(dp, mp), P(mp), P(dp, mp), P(mp, dp))
    return jax.shard_map(
        per_device, mesh=fine, in_specs=in_specs, out_specs=P(dp, mp), check_vma=False
    )
```

```python
import functools

import jax
import jax.numpy as jnp
import numpy as np
from jax import lax
from jax.experimental import pallas as pl
from jax.experimental.pallas import tpu as pltpu
from jax.sharding import Mesh, PartitionSpec as P

epsilon = 1e-06
AXES = ("x", "zt", "zq", "y", "zh", "c")
SIZES = (4, 2, 4, 4, 2, 2)
SIZE = dict(zip(AXES, SIZES))
GAIN_ROWS = 16


def gelu_exact(values):
    return 0.5 * values * (1.0 + lax.erf(values * 0.7071067811865476))


def send(value, axes, k):
    count = int(np.prod([SIZE[a] for a in axes]))
    return lax.ppermute(value, axes, [(i, i ^ k) for i in range(count)])


def after(value, *others):
    return lax.optimization_barrier((value, *others))[0]


def swap_halves(first, second):
    both = [(a, b) for a in (0, 1) for b in (0, 1)]
    straight = lax.ppermute(first, ("zt", "c"), [(2 * a + b, 2 * b + a) for a, b in both])
    crossed = lax.ppermute(second, ("zt", "c"), [(2 * a + b, 2 * b + 1 - a) for a, b in both])
    return straight, crossed


def from_neighbours(value, axis):
    return [send(value, (axis,), k) for k in (1, 3)]


def from_far(one, three, axis, split):
    return send(three[:split], (axis,), 1), send(one[split:], (axis,), 3)


def coordinates():
    return {a: lax.axis_index(a) for a in AXES}


def hidden_kernel(place, mine, other, w0, w1, w2a, w2b, w3, act):
    x, zq, y, zh, c = (place[i] for i in range(5))
    cores = (mine, other)
    rows = act.shape[1]
    width = mine.shape[3]
    count = 2 * mine.shape[0] * 2 * width
    slots = [[w.at[s] for s in range(2)] for w in (w0, w1)] + [[w2a, w2b]] + [[w3.at[s] for s in range(2)]]
    for a in range(2):
        blocks = [(ref, i, 2 * a + j) for ref in cores for i in range(4) for j in range(2)]
        total = jnp.zeros((rows, width), jnp.float32)
        for ref, i, j in blocks:
            total += ref[i, j, :rows, :].astype(jnp.float32)
        center = jnp.sum(total, axis=1, keepdims=True) * (1.0 / count)
        total = jnp.zeros((rows, width), jnp.float32)
        for ref, i, j in blocks:
            total += jnp.square(ref[i, j, :rows, :].astype(jnp.float32) - center)
        spread = jnp.sum(total, axis=1, keepdims=True) * (1.0 / count)
        scale = lax.rsqrt(spread + epsilon)
        acc = jnp.zeros((rows, act.shape[2]), jnp.float32)
        for k in range(4):
            i = x ^ k ^ y
            for s in range(2):
                weights = slots[k][s]
                j = 2 * a + (zh ^ c ^ s)
                for ck, ref in enumerate(cores):
                    first = 2 * (c ^ ck)
                    block = jnp.concatenate(
                        [weights[first ^ zq], weights[(first + 1) ^ zq]], axis=0
                    )
                    gain = ref[i, j, rows : rows + GAIN_ROWS, :].astype(jnp.float32)[0:1]
                    values = ref[i, j, :rows, :].astype(jnp.float32)
                    normed = ((values - center) * scale * gain).astype(jnp.bfloat16)
                    acc += jnp.dot(normed, block, preferred_element_type=jnp.float32)
        act[a] = gelu_exact(acc).astype(act.dtype)


def out_kernel(a, place, act, w0, w1, w2a, w2b, w3, mine, other):
    x, zq, y, zh, c = (place[i] for i in range(5))
    slots = [[w.at[s] for s in range(2)] for w in (w0, w1)] + [[w2a, w2b]] + [[w3.at[s] for s in range(2)]]
    for ck, ref in ((1, other), (0, mine)):
        first = 2 * (c ^ ck)
        for k in range(4):
            for s in range(2):
                weights = slots[k][s]
                block = jnp.concatenate(
                    [weights[first ^ zq], weights[(first + 1) ^ zq]], axis=1
                )
                ref[x ^ k ^ y, zh ^ c ^ s] = jnp.dot(
                    act[a], block, preferred_element_type=jnp.float32
                ).astype(ref.dtype)


def call(kernel, out_shape, flops, *operands):
    vmem = pl.BlockSpec(memory_space=pltpu.VMEM)
    size = sum(o.size * o.dtype.itemsize for o in operands)
    return pl.pallas_call(
        kernel,
        out_shape=out_shape,
        in_specs=[pl.BlockSpec(memory_space=pltpu.SMEM)] + [vmem] * (len(operands) - 1),
        out_specs=jax.tree.map(lambda _: vmem, out_shape),
        compiler_params=pltpu.CompilerParams(vmem_limit_bytes=40 * 1024 * 1024),
        cost_estimate=pl.CostEstimate(flops=flops, bytes_accessed=size, transcendentals=0),
    )(*operands)


def per_device(tokens, norm_gain, w_inner, w_outer):
    at = coordinates()
    zt = at["zt"]
    rows, cols = tokens.shape
    d_dev, f_dev = w_inner.shape
    half = f_dev // 2
    place = jnp.stack([at[a] for a in ("x", "zq", "y", "zh", "c")]).astype(jnp.int32)

    def weight_half(which, axis, array):
        return lax.dynamic_slice_in_dim(array, which * half, half, axis)

    swapped = swap_halves(weight_half(zt, 1, w_inner), weight_half(1 - zt, 1, w_inner))
    both = jnp.concatenate([tokens, jnp.broadcast_to(norm_gain[None], (GAIN_ROWS, cols))], axis=0)
    near = [send(both, ("zt", "zh"), k) for k in (2, 3)]

    inner = after(jnp.stack(swapped), *near)
    inner = jnp.stack([inner] + [send(inner, ("zq",), k) for k in (1, 2, 3)], axis=1)

    in1, in3 = from_neighbours(inner, "x")
    far = send(after(both, inner), ("zt", "zh"), 1)
    swapped = swap_halves(*(weight_half(h, 0, after(w_outer, inner)) for h in (zt, 1 - zt)))

    in2a, in2b = from_far(after(in1, far, *swapped), after(in3, far, *swapped), "x", 1)
    both = after(jnp.stack([both, far] + near), in1, in3, *swapped)
    y1, y3 = from_neighbours(both, "y")
    outer = after(jnp.stack(swapped), in1, in3, far)
    second = send(outer, ("zq",), 2)

    y2a, y2b = from_far(after(y1, in2a, in2b, second), after(y3, in2a, in2b, second), "y", 2)
    pair = send(after(jnp.stack([outer, second], axis=1), in2a, in2b, y1, y3), ("zq",), 1)
    outer = jnp.stack([outer, pair[:, 0], second, pair[:, 1]], axis=1)

    both = jnp.stack([both, y1, jnp.concatenate([y2a, y2b], axis=0), y3])
    out1, out3 = from_neighbours(after(outer, y2a, y2b), "x")
    other = send(after(both, pair), ("c",), 1)

    out2a, out2b = from_far(after(out1, other), out3, "x", 1)

    flops = 2 * 2 * rows * half * 16 * cols
    act = call(
        hidden_kernel,
        jax.ShapeDtypeStruct((2, rows, half), jnp.bfloat16),
        flops, place, both, other, inner, in1, in2a[0], in2b[0], in3,
    )
    shape = jax.ShapeDtypeStruct((4, 2, rows, cols), jnp.bfloat16)
    outer_all = (outer, out1, out2a[0], out2b[0], out3)
    parts = []
    for a in (1, 0):
        mine, other = call(
            functools.partial(out_kernel, a), (shape, shape), flops // 2, place, act, *outer_all
        )
        total = mine.astype(jnp.float32) + send(other, ("c",), 1).astype(jnp.float32)
        sent = total.astype(jnp.bfloat16)
        total = total[0] + sum(send(sent[k], ("y",), k).astype(jnp.float32) for k in (1, 2, 3))
        parts.append((total, total.astype(jnp.bfloat16)))
    (_, away), (total, stay) = parts
    total = total[0] + sum(
        send(piece, ("zt", "zh"), k).astype(jnp.float32)
        for k, piece in ((2, away[0]), (3, away[1]), (1, stay[1]))
    )
    return total.astype(jnp.bfloat16)


def solution(mesh):
    fine = Mesh(np.asarray(mesh.devices).reshape(SIZES), AXES)
    dp, mp = ("x", "zt", "zq"), ("y", "zh", "c")
    in_specs = (P(dp, mp), P(mp), P(dp, mp), P(mp, dp))
    return jax.shard_map(
        per_device, mesh=fine, in_specs=in_specs, out_specs=P(dp, mp), check_vma=False
    )
```

```python
import functools

import jax
import jax.numpy as jnp
import numpy as np
from jax import lax
from jax.experimental import pallas as pl
from jax.experimental.pallas import tpu as pltpu
from jax.sharding import Mesh, PartitionSpec as P

epsilon = 1e-06
AXES = ("x", "zt", "zq", "y", "zh", "c")
SIZES = (4, 2, 4, 4, 2, 2)
SIZE = dict(zip(AXES, SIZES))
GAIN_ROWS = 16


def gelu_exact(values):
    return 0.5 * values * (1.0 + lax.erf(values * 0.7071067811865476))


def send(value, axes, k):
    count = int(np.prod([SIZE[a] for a in axes]))
    return lax.ppermute(value, axes, [(i, i ^ k) for i in range(count)])


def after(value, *others):
    return lax.optimization_barrier((value, *others))[0]


def swap_halves(first, second):
    both = [(a, b) for a in (0, 1) for b in (0, 1)]
    straight = lax.ppermute(first, ("zt", "c"), [(2 * a + b, 2 * b + a) for a, b in both])
    crossed = lax.ppermute(second, ("zt", "c"), [(2 * a + b, 2 * b + 1 - a) for a, b in both])
    return straight, crossed


def from_neighbours(value, axis):
    return [send(value, (axis,), k) for k in (1, 3)]


def from_far(one, three, axis, split):
    return send(three[:split], (axis,), 1), send(one[split:], (axis,), 3)


def coordinates():
    return {a: lax.axis_index(a) for a in AXES}


def hidden_kernel(place, mine, other, w0, w1, w2a, w2b, w3, act):
    x, zq, zt, c = (place[i] for i in (0, 1, 5, 4))
    cores = (mine, other)
    rows = act.shape[1]
    width = mine.shape[2]
    count = mine.shape[0] * width
    slots = [[w.at[s] for s in range(2)] for w in (w0, w1)] + [[w2a, w2b]] + [[w3.at[s] for s in range(2)]]
    for a in range(2):
        blocks = [(ref, 8 * (zt ^ a) + i) for ref in cores for i in range(8)]
        total = jnp.zeros((rows, width), jnp.float32)
        for ref, i in blocks:
            total += ref[i, :rows, :].astype(jnp.float32)
        center = jnp.sum(total, axis=1, keepdims=True) * (1.0 / count)
        total = jnp.zeros((rows, width), jnp.float32)
        for ref, i in blocks:
            total += jnp.square(ref[i, :rows, :].astype(jnp.float32) - center)
        spread = jnp.sum(total, axis=1, keepdims=True) * (1.0 / count)
        scale = lax.rsqrt(spread + epsilon)
        acc = jnp.zeros((rows, act.shape[2]), jnp.float32)
        for k in range(4):
            for s in range(2):
                weights = slots[k][s]
                i = 8 * (zt ^ a) + 2 * (x ^ k) + (c ^ s)
                for ck, ref in enumerate(cores):
                    first = 2 * (c ^ ck)
                    block = jnp.concatenate(
                        [weights[first ^ zq], weights[(first + 1) ^ zq]], axis=0
                    )
                    gain = ref[i, rows : rows + GAIN_ROWS, :].astype(jnp.float32)[0:1]
                    values = ref[i, :rows, :].astype(jnp.float32)
                    normed = ((values - center) * scale * gain).astype(jnp.bfloat16)
                    acc += jnp.dot(normed, block, preferred_element_type=jnp.float32)
        act[a] = gelu_exact(acc).astype(act.dtype)


def out_kernel(a, place, act, w0, w1, w2a, w2b, w3, mine, other):
    x, zq, y, zh, c = (place[i] for i in range(5))
    slots = [[w.at[s] for s in range(2)] for w in (w0, w1)] + [[w2a, w2b]] + [[w3.at[s] for s in range(2)]]
    for ck, ref in ((1, other), (0, mine)):
        first = 2 * (c ^ ck)
        for k in range(4):
            for s in range(2):
                weights = slots[k][s]
                block = jnp.concatenate(
                    [weights[first ^ zq], weights[(first + 1) ^ zq]], axis=1
                )
                ref[x ^ k ^ y, zh ^ c ^ s] = jnp.dot(
                    act[a], block, preferred_element_type=jnp.float32
                ).astype(ref.dtype)


def call(kernel, out_shape, flops, *operands):
    vmem = pl.BlockSpec(memory_space=pltpu.VMEM)
    size = sum(o.size * o.dtype.itemsize for o in operands)
    return pl.pallas_call(
        kernel,
        out_shape=out_shape,
        in_specs=[pl.BlockSpec(memory_space=pltpu.SMEM)] + [vmem] * (len(operands) - 1),
        out_specs=jax.tree.map(lambda _: vmem, out_shape),
        compiler_params=pltpu.CompilerParams(vmem_limit_bytes=40 * 1024 * 1024),
        cost_estimate=pl.CostEstimate(flops=flops, bytes_accessed=size, transcendentals=0),
    )(*operands)


def per_device(tokens, norm_gain, w_inner, w_outer):
    at = coordinates()
    zt = at["zt"]
    rows, cols = tokens.shape
    d_dev, f_dev = w_inner.shape
    half = f_dev // 2
    place = jnp.stack([at[a] for a in ("x", "zq", "y", "zh", "c", "zt")]).astype(jnp.int32)

    def weight_half(which, axis, array):
        return lax.dynamic_slice_in_dim(array, which * half, half, axis)

    both = jnp.concatenate([tokens, jnp.broadcast_to(norm_gain[None], (GAIN_ROWS, cols))], axis=0)
    both = lax.all_gather(both, ("zt", "y", "zh"))

    in_swapped = swap_halves(weight_half(zt, 1, w_inner), weight_half(1 - zt, 1, w_inner))
    out_swapped = swap_halves(weight_half(zt, 0, w_outer), weight_half(1 - zt, 0, w_outer))

    inner = jnp.stack(in_swapped)
    others = [send(inner, ("zq",), k) for k in (2, 3)]
    others = [send(after(inner, *out_swapped), ("zq",), 1)] + others
    inner = jnp.stack([inner] + others, axis=1)

    in1, in3 = from_neighbours(inner, "x")
    outer = after(jnp.stack(out_swapped), inner)
    outer = jnp.stack([outer] + [send(outer, ("zq",), k) for k in (1, 2, 3)], axis=1)

    in2a, in2b = from_far(after(in1, outer), after(in3, outer), "x", 1)
    out1, out3 = from_neighbours(after(outer, in1, in3), "x")
    other = send(after(both, out1, out3), ("c",), 1)

    out2a, out2b = from_far(after(out1, in2a, in2b), out3, "x", 1)

    flops = 2 * 2 * rows * half * 16 * cols
    act = call(
        hidden_kernel,
        jax.ShapeDtypeStruct((2, rows, half), jnp.bfloat16),
        flops, place, both, other, inner, in1, in2a[0], in2b[0], in3,
    )
    shape = jax.ShapeDtypeStruct((4, 2, rows, cols), jnp.bfloat16)
    outer_all = (outer, out1, out2a[0], out2b[0], out3)
    parts = []
    for a in (1, 0):
        mine, other = call(
            functools.partial(out_kernel, a), (shape, shape), flops // 2, place, act, *outer_all
        )
        total = mine.astype(jnp.float32) + send(other, ("c",), 1).astype(jnp.float32)
        sent = total.astype(jnp.bfloat16)
        total = total[0] + sum(send(sent[k], ("y",), k).astype(jnp.float32) for k in (1, 2, 3))
        parts.append((total, total.astype(jnp.bfloat16)))
        act = after(act, other)
    (_, away), (total, stay) = parts
    total = total[0] + sum(
        send(piece, ("zt", "zh"), k).astype(jnp.float32)
        for k, piece in ((2, away[0]), (3, away[1]), (1, stay[1]))
    )
    return total.astype(jnp.bfloat16)


def solution(mesh):
    fine = Mesh(np.asarray(mesh.devices).reshape(SIZES), AXES)
    dp, mp = ("x", "zt", "zq"), ("y", "zh", "c")
    in_specs = (P(dp, mp), P(mp), P(dp, mp), P(mp, dp))
    return jax.shard_map(
        per_device, mesh=fine, in_specs=in_specs, out_specs=P(dp, mp), check_vma=False
    )
```

```python
import functools

import jax
import jax.numpy as jnp
import numpy as np
from jax import lax
from jax.experimental import pallas as pl
from jax.experimental.pallas import tpu as pltpu
from jax.sharding import Mesh, PartitionSpec as P

epsilon = 1e-06
AXES = ("x", "zt", "zq", "y", "zh", "c")
SIZES = (4, 2, 4, 4, 2, 2)
SIZE = dict(zip(AXES, SIZES))
GAIN_ROWS = 16


def gelu_exact(values):
    return 0.5 * values * (1.0 + lax.erf(values * 0.7071067811865476))


def send(value, axes, k):
    count = int(np.prod([SIZE[a] for a in axes]))
    return lax.ppermute(value, axes, [(i, i ^ k) for i in range(count)])


def after(value, *others):
    return lax.optimization_barrier((value, *others))[0]


def swap_halves(first, second):
    both = [(a, b) for a in (0, 1) for b in (0, 1)]
    straight = lax.ppermute(first, ("zt", "c"), [(2 * a + b, 2 * b + a) for a, b in both])
    crossed = lax.ppermute(second, ("zt", "c"), [(2 * a + b, 2 * b + 1 - a) for a, b in both])
    return straight, crossed


def from_neighbours(value, axis):
    return [send(value, (axis,), k) for k in (1, 3)]


def from_far(one, three, axis, split):
    return send(three[:split], (axis,), 1), send(one[split:], (axis,), 3)


def coordinates():
    return {a: lax.axis_index(a) for a in AXES}


def hidden_kernel(place, mine, other, w0, w1, w2a, w2b, w3, act):
    x, zq, y, zh, c = (place[i] for i in range(5))
    cores = (mine, other)
    rows = act.shape[1]
    width = mine.shape[3]
    count = 2 * mine.shape[0] * 2 * width
    slots = [[w.at[s] for s in range(2)] for w in (w0, w1)] + [[w2a, w2b]] + [[w3.at[s] for s in range(2)]]
    for a in range(2):
        blocks = [(ref, i, 2 * a + j) for ref in cores for i in range(4) for j in range(2)]
        total = jnp.zeros((rows, width), jnp.float32)
        for ref, i, j in blocks:
            total += ref[i, j, :rows, :].astype(jnp.float32)
        center = jnp.sum(total, axis=1, keepdims=True) * (1.0 / count)
        total = jnp.zeros((rows, width), jnp.float32)
        for ref, i, j in blocks:
            total += jnp.square(ref[i, j, :rows, :].astype(jnp.float32) - center)
        spread = jnp.sum(total, axis=1, keepdims=True) * (1.0 / count)
        scale = lax.rsqrt(spread + epsilon)
        acc = jnp.zeros((rows, act.shape[2]), jnp.float32)
        for k in range(4):
            i = x ^ k ^ y
            for s in range(2):
                weights = slots[k][s]
                j = 2 * a + (zh ^ c ^ s)
                for ck, ref in enumerate(cores):
                    first = 2 * (c ^ ck)
                    block = jnp.concatenate(
                        [weights[first ^ zq], weights[(first + 1) ^ zq]], axis=0
                    )
                    gain = ref[i, j, rows : rows + GAIN_ROWS, :].astype(jnp.float32)[0:1]
                    values = ref[i, j, :rows, :].astype(jnp.float32)
                    normed = ((values - center) * scale * gain).astype(jnp.bfloat16)
                    acc += jnp.dot(normed, block, preferred_element_type=jnp.float32)
        act[a] = gelu_exact(acc).astype(act.dtype)


def out_kernel(a, place, act, w0, w1, w2a, w2b, w3, mine, other):
    x, zq, y, zh, c = (place[i] for i in range(5))
    slots = [[w.at[s] for s in range(2)] for w in (w0, w1)] + [[w2a, w2b]] + [[w3.at[s] for s in range(2)]]
    for ck, ref in ((1, other), (0, mine)):
        first = 2 * (c ^ ck)
        for k in range(4):
            for s in range(2):
                weights = slots[k][s]
                block = jnp.concatenate(
                    [weights[first ^ zq], weights[(first + 1) ^ zq]], axis=1
                )
                ref[x ^ k ^ y, zh ^ c ^ s] = jnp.dot(
                    act[a], block, preferred_element_type=jnp.float32
                ).astype(ref.dtype)


def call(kernel, out_shape, flops, *operands):
    vmem = pl.BlockSpec(memory_space=pltpu.VMEM)
    size = sum(o.size * o.dtype.itemsize for o in operands)
    return pl.pallas_call(
        kernel,
        out_shape=out_shape,
        in_specs=[pl.BlockSpec(memory_space=pltpu.SMEM)] + [vmem] * (len(operands) - 1),
        out_specs=jax.tree.map(lambda _: vmem, out_shape),
        compiler_params=pltpu.CompilerParams(vmem_limit_bytes=40 * 1024 * 1024),
        cost_estimate=pl.CostEstimate(flops=flops, bytes_accessed=size, transcendentals=0),
    )(*operands)


def per_device(tokens, norm_gain, w_inner, w_outer):
    at = coordinates()
    zt = at["zt"]
    rows, cols = tokens.shape
    d_dev, f_dev = w_inner.shape
    half = f_dev // 2
    place = jnp.stack([at[a] for a in ("x", "zq", "y", "zh", "c")]).astype(jnp.int32)

    def weight_half(which, axis, array):
        return lax.dynamic_slice_in_dim(array, which * half, half, axis)

    both = jnp.concatenate([tokens, jnp.broadcast_to(norm_gain[None], (GAIN_ROWS, cols))], axis=0)
    both = jnp.stack([both] + [send(both, ("zt", "zh"), k) for k in (1, 2, 3)])
    swapped = swap_halves(weight_half(zt, 1, w_inner), weight_half(1 - zt, 1, w_inner))

    inner = after(jnp.stack(swapped), both)
    both = after(both, *swapped)
    inner = jnp.stack([inner] + [send(inner, ("zq",), k) for k in (1, 2, 3)], axis=1)
    y1, y3 = from_neighbours(both, "y")

    in1, in3 = from_neighbours(after(inner, y1, y3), "x")
    swapped = swap_halves(*(weight_half(h, 0, after(w_outer, inner, y1, y3)) for h in (zt, 1 - zt)))
    y2 = send(after(both, inner, y1, y3), ("y",), 2)
    both = jnp.stack([both, y1, y2, y3])

    in2a, in2b = from_far(after(in1, y2, *swapped), after(in3, y2, *swapped), "x", 1)
    other = send(after(both, in1, in3, *swapped), ("c",), 1)
    outer = after(jnp.stack(swapped), in1, in3, y2)
    outer = jnp.stack([outer] + [send(outer, ("zq",), k) for k in (1, 2, 3)], axis=1)

    out1, out3 = from_neighbours(after(outer, in2a, in2b, other), "x")

    flops = 2 * 2 * rows * half * 16 * cols
    act = call(
        hidden_kernel,
        jax.ShapeDtypeStruct((2, rows, half), jnp.bfloat16),
        flops, place, both, other, inner, in1, in2a[0], in2b[0], in3,
    )
    out2a, out2b = from_far(after(out1, act), after(out3, act), "x", 1)
    shape = jax.ShapeDtypeStruct((4, 2, rows, cols), jnp.bfloat16)
    outer_all = (outer, out1, out2a[0], out2b[0], out3)
    parts = []
    for a in (0, 1):
        mine, other = call(
            functools.partial(out_kernel, a), (shape, shape), flops // 2, place, act, *outer_all
        )
        total = mine.astype(jnp.float32) + send(other, ("c",), 1).astype(jnp.float32)
        sent = total.astype(jnp.bfloat16)
        total = total[0] + sum(send(sent[k], ("y",), k).astype(jnp.float32) for k in (1, 2, 3))
        parts.append((total, total.astype(jnp.bfloat16)))
    (total, stay), (_, away) = parts
    total = total[0] + sum(
        send(piece, ("zt", "zh"), k).astype(jnp.float32)
        for k, piece in ((2, away[0]), (3, away[1]), (1, stay[1]))
    )
    return total.astype(jnp.bfloat16)


def solution(mesh):
    fine = Mesh(np.asarray(mesh.devices).reshape(SIZES), AXES)
    dp, mp = ("x", "zt", "zq"), ("y", "zh", "c")
    in_specs = (P(dp, mp), P(mp), P(dp, mp), P(mp, dp))
    return jax.shard_map(
        per_device, mesh=fine, in_specs=in_specs, out_specs=P(dp, mp), check_vma=False
    )
```

```python
import functools

import jax
import jax.numpy as jnp
import numpy as np
from jax import lax
from jax.experimental import pallas as pl
from jax.experimental.pallas import tpu as pltpu
from jax.sharding import Mesh, PartitionSpec as P

epsilon = 1e-06
AXES = ("x", "zt", "zq", "y", "zh", "c")
SIZES = (4, 2, 4, 4, 2, 2)
SIZE = dict(zip(AXES, SIZES))
GAIN_ROWS = 16


def gelu_exact(values):
    return 0.5 * values * (1.0 + lax.erf(values * 0.7071067811865476))


def send(value, axes, k):
    count = int(np.prod([SIZE[a] for a in axes]))
    return lax.ppermute(value, axes, [(i, i ^ k) for i in range(count)])


def after(value, *others):
    return lax.optimization_barrier((value, *others))[0]


def swap_halves(first, second):
    both = [(a, b) for a in (0, 1) for b in (0, 1)]
    straight = lax.ppermute(first, ("zt", "c"), [(2 * a + b, 2 * b + a) for a, b in both])
    crossed = lax.ppermute(second, ("zt", "c"), [(2 * a + b, 2 * b + 1 - a) for a, b in both])
    return straight, crossed


def from_neighbours(value, axis):
    return [send(value, (axis,), k) for k in (1, 3)]


def from_far(one, three, axis, split):
    return send(three[:split], (axis,), 1), send(one[split:], (axis,), 3)


def coordinates():
    return {a: lax.axis_index(a) for a in AXES}


def hidden_kernel(place, *refs):
    far, act, held, sems = refs[:7], refs[7], refs[8:15], refs[15]
    x, zq, y, zh, c = (place[i] for i in range(5))
    copies = []
    for i in range(far[0].shape[0]):
        for ref, near in zip(far[:2], held[:2]):
            copies.append(pltpu.make_async_copy(ref.at[i], near.at[i], sems.at[len(copies)]))
    for ref, near in zip(far[2:], held[2:]):
        copies.append(pltpu.make_async_copy(ref, near, sems.at[len(copies)]))
    for copy in copies:
        copy.start()
    mine, other, w0, w1, w2a, w2b, w3 = held
    cores = (mine, other)
    rows = act.shape[1]
    width = mine.shape[3]
    count = 2 * mine.shape[0] * 2 * width
    slots = [[w.at[s] for s in range(2)] for w in (w0, w1)] + [[w2a, w2b]] + [[w3.at[s] for s in range(2)]]
    for copy in copies[:8]:
        copy.wait()
    norms = []
    for a in range(2):
        blocks = [(ref, i, 2 * a + j) for i in range(4) for ref in cores for j in range(2)]
        total = jnp.zeros((rows, width), jnp.float32)
        for ref, i, j in blocks:
            total += ref[i, j, :rows, :].astype(jnp.float32)
        center = jnp.sum(total, axis=1, keepdims=True) * (1.0 / count)
        total = jnp.zeros((rows, width), jnp.float32)
        for ref, i, j in blocks:
            total += jnp.square(ref[i, j, :rows, :].astype(jnp.float32) - center)
        spread = jnp.sum(total, axis=1, keepdims=True) * (1.0 / count)
        norms.append((center, lax.rsqrt(spread + epsilon)))
    for copy in copies[8:]:
        copy.wait()
    for a, (center, scale) in enumerate(norms):
        acc = jnp.zeros((rows, act.shape[2]), jnp.float32)
        for k in range(4):
            i = x ^ k ^ y
            for s in range(2):
                weights = slots[k][s]
                j = 2 * a + (zh ^ c ^ s)
                for ck, ref in enumerate(cores):
                    first = 2 * (c ^ ck)
                    block = jnp.concatenate(
                        [weights[first ^ zq], weights[(first + 1) ^ zq]], axis=0
                    )
                    gain = ref[i, j, rows : rows + GAIN_ROWS, :].astype(jnp.float32)[0:1]
                    values = ref[i, j, :rows, :].astype(jnp.float32)
                    normed = ((values - center) * scale * gain).astype(jnp.bfloat16)
                    acc += jnp.dot(normed, block, preferred_element_type=jnp.float32)
        act[a] = gelu_exact(acc).astype(act.dtype)


def out_kernel(a, place, act, w0, w1, w2a, w2b, w3, mine, other):
    x, zq, y, zh, c = (place[i] for i in range(5))
    slots = [[w.at[s] for s in range(2)] for w in (w0, w1)] + [[w2a, w2b]] + [[w3.at[s] for s in range(2)]]
    for ck, ref in ((1, other), (0, mine)):
        first = 2 * (c ^ ck)
        for k in range(4):
            for s in range(2):
                weights = slots[k][s]
                block = jnp.concatenate(
                    [weights[first ^ zq], weights[(first + 1) ^ zq]], axis=1
                )
                ref[x ^ k ^ y, zh ^ c ^ s] = jnp.dot(
                    act[a], block, preferred_element_type=jnp.float32
                ).astype(ref.dtype)


def call(kernel, out_shape, flops, *operands, copied=False):
    vmem = pl.BlockSpec(memory_space=pltpu.VMEM)
    given = pl.BlockSpec(memory_space=pltpu.HBM) if copied else vmem
    size = sum(o.size * o.dtype.itemsize for o in operands)
    scratch = [pltpu.VMEM(o.shape, o.dtype) for o in operands[1:]]
    return pl.pallas_call(
        kernel,
        out_shape=out_shape,
        in_specs=[pl.BlockSpec(memory_space=pltpu.SMEM)] + [given] * (len(operands) - 1),
        out_specs=jax.tree.map(lambda _: vmem, out_shape),
        scratch_shapes=scratch + [pltpu.SemaphoreType.DMA((16,))] if copied else [],
        compiler_params=pltpu.CompilerParams(vmem_limit_bytes=40 * 1024 * 1024),
        cost_estimate=pl.CostEstimate(flops=flops, bytes_accessed=size, transcendentals=0),
    )(*operands)


def per_device(tokens, norm_gain, w_inner, w_outer):
    at = coordinates()
    zt = at["zt"]
    rows, cols = tokens.shape
    d_dev, f_dev = w_inner.shape
    half = f_dev // 2
    place = jnp.stack([at[a] for a in ("x", "zq", "y", "zh", "c")]).astype(jnp.int32)

    def weight_half(which, axis, array):
        return lax.dynamic_slice_in_dim(array, which * half, half, axis)

    both = jnp.concatenate([tokens, jnp.broadcast_to(norm_gain[None], (GAIN_ROWS, cols))], axis=0)
    both = jnp.stack([both] + [send(both, ("zt", "zh"), k) for k in (1, 2, 3)])
    swapped = swap_halves(weight_half(zt, 1, w_inner), weight_half(1 - zt, 1, w_inner))

    inner = after(jnp.stack(swapped), both)
    inner = jnp.stack([inner] + [send(inner, ("zq",), k) for k in (1, 2, 3)], axis=1)

    in1, in3 = from_neighbours(inner, "x")
    swapped = swap_halves(*(weight_half(h, 0, after(w_outer, inner)) for h in (zt, 1 - zt)))
    y1 = send(after(both, inner), ("y",), 1)
    outer = jnp.stack(swapped)
    second = send(outer, ("zq",), 2)
    y3 = send(after(both, y1, *swapped), ("y",), 3)

    in2a, in2b = from_far(after(in1, second, y1), after(in3, second, y1), "x", 1)
    pair = send(after(jnp.stack([outer, second], axis=1), in1, in3), ("zq",), 1)
    outer = jnp.stack([outer, pair[:, 0], second, pair[:, 1]], axis=1)
    y2 = send(after(both, in1, in3, y3, second), ("y",), 2)

    out1, out3 = from_neighbours(after(outer, in2a, in2b, y3), "x")
    both = jnp.stack([both, y1, y2, y3])
    other = send(after(both, outer, in2a, in2b), ("c",), 1)

    out2a, out2b = from_far(after(out1, other), after(out3, other), "x", 1)

    flops = 2 * 2 * rows * half * 16 * cols
    act = call(
        hidden_kernel,
        jax.ShapeDtypeStruct((2, rows, half), jnp.bfloat16),
        flops, place, both, other, inner, in1, in2a[0], in2b[0], in3, copied=True,
    )
    shape = jax.ShapeDtypeStruct((4, 2, rows, cols), jnp.bfloat16)
    outer_all = (outer, out1, out2a[0], out2b[0], out3)
    parts = []
    for a in (0, 1):
        mine, other = call(
            functools.partial(out_kernel, a), (shape, shape), flops // 2, place, act, *outer_all
        )
        total = mine.astype(jnp.float32) + send(other, ("c",), 1).astype(jnp.float32)
        sent = total.astype(jnp.bfloat16)
        total = total[0] + sum(send(sent[k], ("y",), k).astype(jnp.float32) for k in (1, 2, 3))
        parts.append((total, total.astype(jnp.bfloat16)))
    (total, stay), (_, away) = parts
    total = total[0] + sum(
        send(piece, ("zt", "zh"), k).astype(jnp.float32)
        for k, piece in ((2, away[0]), (3, away[1]), (1, stay[1]))
    )
    return total.astype(jnp.bfloat16)


def solution(mesh):
    fine = Mesh(np.asarray(mesh.devices).reshape(SIZES), AXES)
    dp, mp = ("x", "zt", "zq"), ("y", "zh", "c")
    in_specs = (P(dp, mp), P(mp), P(dp, mp), P(mp, dp))
    return jax.shard_map(
        per_device, mesh=fine, in_specs=in_specs, out_specs=P(dp, mp), check_vma=False
    )
```

```python
import functools

import jax
import jax.numpy as jnp
import numpy as np
from jax import lax
from jax.experimental import pallas as pl
from jax.experimental.pallas import tpu as pltpu
from jax.sharding import Mesh, PartitionSpec as P

epsilon = 1e-06
AXES = ("x", "zt", "zq", "y", "zh", "c")
SIZES = (4, 2, 4, 4, 2, 2)
SIZE = dict(zip(AXES, SIZES))
GAIN_ROWS = 16


def gelu_exact(values):
    return 0.5 * values * (1.0 + lax.erf(values * 0.7071067811865476))


def send(value, axes, k):
    count = int(np.prod([SIZE[a] for a in axes]))
    return lax.ppermute(value, axes, [(i, i ^ k) for i in range(count)])


def after(value, *others):
    return lax.optimization_barrier((value, *others))[0]


def swap_halves(first, second):
    both = [(a, b) for a in (0, 1) for b in (0, 1)]
    straight = lax.ppermute(first, ("zt", "c"), [(2 * a + b, 2 * b + a) for a, b in both])
    crossed = lax.ppermute(second, ("zt", "c"), [(2 * a + b, 2 * b + 1 - a) for a, b in both])
    return straight, crossed


def from_neighbours(value, axis):
    return [send(value, (axis,), k) for k in (1, 3)]


def from_far(one, three, axis, split):
    return send(three[:split], (axis,), 1), send(one[split:], (axis,), 3)


def swap_blocks(block):
    place = [(a, q) for a in range(2) for q in range(4)]
    axes = ("zt", "zq", "c")
    own = [(8 * a + 2 * q + a, 8 * a + 2 * q + q // 2) for a, q in place]
    own += [(8 * a + 2 * q + 1 - a, 8 * a + 2 * q + 1 - q // 2) for a, q in place]
    cross = [(8 * a + 2 * q + 1 - a, 8 * (1 - a) + 2 * q + q // 2) for a, q in place]
    cross += [(8 * a + 2 * q + a, 8 * a + 2 * q + 1 - q // 2) for a, q in place]
    return lax.ppermute(block, axes, own), lax.ppermute(block, axes, cross)


def spread_blocks(blocks, at):
    got = []
    for k in (1, 2, 3):
        pairs = [(2 * q + q // 2, 2 * (q ^ k) + q // 2) for q in range(4)]
        pairs += [(2 * q + 1 - q // 2, 2 * q + (q // 2 + (k == 1)) % 2) for q in range(4)]
        got.append(lax.ppermute(blocks, ("zq", "c"), pairs))
    one, two, three = got
    here = at["zq"] // 2 == at["c"]
    return jnp.stack([jnp.where(here, blocks, two), jnp.where(here, one, three)], axis=1)


def coordinates():
    return {a: lax.axis_index(a) for a in AXES}


def hidden_kernel(place, *refs):
    far, act, held, sems = refs[:7], refs[7], refs[8:15], refs[15]
    x, zq, y, zh, c = (place[i] for i in range(5))
    copies = []
    for i in range(far[0].shape[0]):
        for ref, near in zip(far[:2], held[:2]):
            copies.append(pltpu.make_async_copy(ref.at[i], near.at[i], sems.at[len(copies)]))
    for ref, near in zip(far[2:], held[2:]):
        copies.append(pltpu.make_async_copy(ref, near, sems.at[len(copies)]))
    for copy in copies:
        copy.start()
    mine, other, w0, w1, w2a, w2b, w3 = held
    cores = (mine, other)
    rows = act.shape[1]
    width = mine.shape[3]
    count = 2 * mine.shape[0] * 2 * width
    slots = [[w.at[s] for s in range(2)] for w in (w0, w1)] + [[w2a, w2b]] + [[w3.at[s] for s in range(2)]]
    for copy in copies[:8]:
        copy.wait()
    norms = []
    for a in range(2):
        blocks = [(ref, i, 2 * a + j) for i in range(4) for ref in cores for j in range(2)]
        total = jnp.zeros((rows, width), jnp.float32)
        for ref, i, j in blocks:
            total += ref[i, j, :rows, :].astype(jnp.float32)
        center = jnp.sum(total, axis=1, keepdims=True) * (1.0 / count)
        total = jnp.zeros((rows, width), jnp.float32)
        for ref, i, j in blocks:
            total += jnp.square(ref[i, j, :rows, :].astype(jnp.float32) - center)
        spread = jnp.sum(total, axis=1, keepdims=True) * (1.0 / count)
        norms.append((center, lax.rsqrt(spread + epsilon)))
    for copy in copies[8:]:
        copy.wait()
    for a, (center, scale) in enumerate(norms):
        acc = jnp.zeros((rows, act.shape[2]), jnp.float32)
        for k in range(4):
            i = x ^ k ^ y
            for s in range(2):
                weights = slots[k][s]
                j = 2 * a + (zh ^ c ^ s)
                for ck, ref in enumerate(cores):
                    first = 2 * (c ^ ck)
                    block = jnp.concatenate(
                        [weights[first ^ zq], weights[(first + 1) ^ zq]], axis=0
                    )
                    gain = ref[i, j, rows : rows + GAIN_ROWS, :].astype(jnp.float32)[0:1]
                    values = ref[i, j, :rows, :].astype(jnp.float32)
                    normed = ((values - center) * scale * gain).astype(jnp.bfloat16)
                    acc += jnp.dot(normed, block, preferred_element_type=jnp.float32)
        act[a] = gelu_exact(acc).astype(act.dtype)


def out_kernel(a, place, act, act_other, w0, w1, w2a, w2b, w3, out):
    x, zq, y, zh, c, zt = (place[i] for i in range(6))
    half = act.shape[2]
    slots = [[w.at[s] for s in range(2)] for w in (w0, w1)] + [[w2a, w2b]] + [[w3.at[s] for s in range(2)]]
    for k in range(4):
        for s in range(2):
            total = None
            for core, part in ((c, act), (1 - c, act_other)):
                units = pl.ds(pl.multiple_of(core * half, half), half)
                block = jnp.concatenate(
                    [slots[k][s][zq & 1, units, :], slots[k][s][1 - (zq & 1), units, :]], axis=1
                )
                term = jnp.dot(part[a], block, preferred_element_type=jnp.float32)
                total = term if total is None else total + term
            out[x ^ k ^ y, zh ^ zt ^ s] = total.astype(out.dtype)


def call(kernel, out_shape, flops, *operands, copied=False):
    vmem = pl.BlockSpec(memory_space=pltpu.VMEM)
    given = pl.BlockSpec(memory_space=pltpu.HBM) if copied else vmem
    size = sum(o.size * o.dtype.itemsize for o in operands)
    scratch = [pltpu.VMEM(o.shape, o.dtype) for o in operands[1:]]
    return pl.pallas_call(
        kernel,
        out_shape=out_shape,
        in_specs=[pl.BlockSpec(memory_space=pltpu.SMEM)] + [given] * (len(operands) - 1),
        out_specs=jax.tree.map(lambda _: vmem, out_shape),
        scratch_shapes=scratch + [pltpu.SemaphoreType.DMA((16,))] if copied else [],
        compiler_params=pltpu.CompilerParams(vmem_limit_bytes=40 * 1024 * 1024),
        cost_estimate=pl.CostEstimate(flops=flops, bytes_accessed=size, transcendentals=0),
    )(*operands)


def per_device(tokens, norm_gain, w_inner, w_outer):
    at = coordinates()
    zt = at["zt"]
    rows, cols = tokens.shape
    d_dev, f_dev = w_inner.shape
    half = f_dev // 2
    place = jnp.stack([at[a] for a in ("x", "zq", "y", "zh", "c", "zt")]).astype(jnp.int32)

    def weight_half(which, axis, array):
        return lax.dynamic_slice_in_dim(array, which * half, half, axis)

    both = jnp.concatenate([tokens, jnp.broadcast_to(norm_gain[None], (GAIN_ROWS, cols))], axis=0)
    both = jnp.stack([both] + [send(both, ("zt", "zh"), k) for k in (1, 2, 3)])
    swapped = swap_halves(weight_half(zt, 1, w_inner), weight_half(1 - zt, 1, w_inner))

    inner = after(jnp.stack(swapped), both)
    both = after(both, *swapped)
    inner = jnp.stack([inner] + [send(inner, ("zq",), k) for k in (1, 2, 3)], axis=1)
    y1, y3 = from_neighbours(both, "y")

    in1, in3 = from_neighbours(after(inner, y1, y3), "x")
    swapped = swap_blocks(after(w_outer, inner, y1, y3))
    y2 = send(after(both, inner, y1, y3), ("y",), 2)

    in2a, in2b = from_far(after(in1, y2, *swapped), after(in3, y2, *swapped), "x", 1)
    outer = spread_blocks(after(jnp.stack(swapped), in1, in3, y2), at)

    out1, out3 = from_neighbours(after(outer, in2a, in2b), "x")
    both = jnp.stack([both, y1, y2, y3])
    other = send(after(both, outer, in2a, in2b), ("c",), 1)

    out2a, out2b = from_far(after(out1, other), after(out3, other), "x", 1)

    flops = 2 * 2 * rows * half * 16 * cols
    act = call(
        hidden_kernel,
        jax.ShapeDtypeStruct((2, rows, half), jnp.bfloat16),
        flops, place, both, other, inner, in1, in2a[0], in2b[0], in3, copied=True,
    )
    act_other = send(act, ("c",), 1)
    shape = jax.ShapeDtypeStruct((4, 2, rows, cols), jnp.bfloat16)
    parts = []
    for a in (0, 1):
        sent = call(
            functools.partial(out_kernel, a), shape, flops // 2,
            place, act, act_other, outer, out1, out2a[0], out2b[0], out3,
        )
        total = sent[0].astype(jnp.float32) + sum(
            send(sent[k], ("y",), k).astype(jnp.float32) for k in (1, 2, 3)
        )
        parts.append((total, total.astype(jnp.bfloat16)))
    (total, stay), (_, away) = parts
    total = total[0] + sum(
        send(piece, ("zt", "zh"), k).astype(jnp.float32)
        for k, piece in ((2, away[0]), (3, away[1]), (1, stay[1]))
    )
    return total.astype(jnp.bfloat16)


def solution(mesh):
    fine = Mesh(np.asarray(mesh.devices).reshape(SIZES), AXES)
    dp, mp = ("x", "zt", "zq"), ("y", "zh", "c")
    in_specs = (P(dp, mp), P(mp), P(dp, mp), P(mp, dp))
    return jax.shard_map(
        per_device, mesh=fine, in_specs=in_specs, out_specs=P(dp, mp), check_vma=False
    )
```

```python
import functools

import jax
import jax.numpy as jnp
import numpy as np
from jax import lax
from jax.experimental import pallas as pl
from jax.experimental.pallas import tpu as pltpu
from jax.sharding import Mesh, PartitionSpec as P

epsilon = 1e-06
AXES = ("x", "zt", "zq", "y", "zh", "c")
SIZES = (4, 2, 4, 4, 2, 2)
SIZE = dict(zip(AXES, SIZES))
GAIN_ROWS = 16


def gelu_exact(values):
    return 0.5 * values * (1.0 + lax.erf(values * 0.7071067811865476))


def send(value, axes, k):
    count = int(np.prod([SIZE[a] for a in axes]))
    return lax.ppermute(value, axes, [(i, i ^ k) for i in range(count)])


def after(value, *others):
    return lax.optimization_barrier((value, *others))[0]


def swap_halves(first, second):
    both = [(a, b) for a in (0, 1) for b in (0, 1)]
    straight = lax.ppermute(first, ("zt", "c"), [(2 * a + b, 2 * b + a) for a, b in both])
    crossed = lax.ppermute(second, ("zt", "c"), [(2 * a + b, 2 * b + 1 - a) for a, b in both])
    return straight, crossed


def from_neighbours(value, axis):
    return [send(value, (axis,), k) for k in (1, 3)]


def from_far(one, three, axis, split):
    return send(three[:split], (axis,), 1), send(one[split:], (axis,), 3)


def swap_blocks(block):
    place = [(a, q) for a in range(2) for q in range(4)]
    axes = ("zt", "zq", "c")
    own = [(8 * a + 2 * q + a, 8 * a + 2 * q + q // 2) for a, q in place]
    own += [(8 * a + 2 * q + 1 - a, 8 * a + 2 * q + 1 - q // 2) for a, q in place]
    cross = [(8 * a + 2 * q + 1 - a, 8 * (1 - a) + 2 * q + q // 2) for a, q in place]
    cross += [(8 * a + 2 * q + a, 8 * a + 2 * q + 1 - q // 2) for a, q in place]
    return lax.ppermute(block, axes, own), lambda block: lax.ppermute(block, axes, cross)


def spread_blocks(blocks, at):
    got = []
    for k in (1, 2, 3):
        pairs = [(2 * q + q // 2, 2 * (q ^ k) + q // 2) for q in range(4)]
        pairs += [(2 * q + 1 - q // 2, 2 * q + (q // 2 + (k == 1)) % 2) for q in range(4)]
        got.append(lax.ppermute(blocks, ("zq", "c"), pairs))
    one, two, three = got
    here = at["zq"] // 2 == at["c"]
    return jnp.stack([jnp.where(here, blocks, two), jnp.where(here, one, three)], axis=1)


def coordinates():
    return {a: lax.axis_index(a) for a in AXES}


def hidden_kernel(place, *refs):
    far, act, held, sems = refs[:7], refs[7], refs[8:15], refs[15]
    x, zq, y, zh, c = (place[i] for i in range(5))
    copies = []
    for i in range(far[0].shape[0]):
        for ref, near in zip(far[:2], held[:2]):
            copies.append(pltpu.make_async_copy(ref.at[i], near.at[i], sems.at[len(copies)]))
    for ref, near in zip(far[2:], held[2:]):
        copies.append(pltpu.make_async_copy(ref, near, sems.at[len(copies)]))
    for copy in copies:
        copy.start()
    mine, other, w0, w1, w2a, w2b, w3 = held
    cores = (mine, other)
    rows = act.shape[1]
    width = mine.shape[3]
    count = 2 * mine.shape[0] * 2 * width
    slots = [[w.at[s] for s in range(2)] for w in (w0, w1)] + [[w2a, w2b]] + [[w3.at[s] for s in range(2)]]
    for copy in copies[:8]:
        copy.wait()
    norms = []
    for a in range(2):
        blocks = [(ref, i, 2 * a + j) for i in range(4) for ref in cores for j in range(2)]
        total = jnp.zeros((rows, width), jnp.float32)
        for ref, i, j in blocks:
            total += ref[i, j, :rows, :].astype(jnp.float32)
        center = jnp.sum(total, axis=1, keepdims=True) * (1.0 / count)
        total = jnp.zeros((rows, width), jnp.float32)
        for ref, i, j in blocks:
            total += jnp.square(ref[i, j, :rows, :].astype(jnp.float32) - center)
        spread = jnp.sum(total, axis=1, keepdims=True) * (1.0 / count)
        norms.append((center, lax.rsqrt(spread + epsilon)))
    for copy in copies[8:]:
        copy.wait()
    for a, (center, scale) in enumerate(norms):
        acc = jnp.zeros((rows, act.shape[2]), jnp.float32)
        for k in range(4):
            i = x ^ k ^ y
            for s in range(2):
                weights = slots[k][s]
                j = 2 * a + (zh ^ c ^ s)
                for ck, ref in enumerate(cores):
                    first = 2 * (c ^ ck)
                    block = jnp.concatenate(
                        [weights[first ^ zq], weights[(first + 1) ^ zq]], axis=0
                    )
                    gain = ref[i, j, rows : rows + GAIN_ROWS, :].astype(jnp.float32)[0:1]
                    values = ref[i, j, :rows, :].astype(jnp.float32)
                    normed = ((values - center) * scale * gain).astype(jnp.bfloat16)
                    acc += jnp.dot(normed, block, preferred_element_type=jnp.float32)
        act[a] = gelu_exact(acc).astype(act.dtype)


def out_kernel(a, place, act, act_other, w0, w1, w2a, w2b, w3, out):
    x, zq, y, zh, c, zt = (place[i] for i in range(6))
    half = act.shape[2]
    slots = [[w.at[s] for s in range(2)] for w in (w0, w1)] + [[w2a, w2b]] + [[w3.at[s] for s in range(2)]]
    for k in range(4):
        for s in range(2):
            total = None
            for core, part in ((c, act), (1 - c, act_other)):
                units = pl.ds(pl.multiple_of(core * half, half), half)
                block = jnp.concatenate(
                    [slots[k][s][zq & 1, units, :], slots[k][s][1 - (zq & 1), units, :]], axis=1
                )
                term = jnp.dot(part[a], block, preferred_element_type=jnp.float32)
                total = term if total is None else total + term
            out[x ^ k ^ y, zh ^ zt ^ s] = total.astype(out.dtype)


def call(kernel, out_shape, flops, *operands, copied=False):
    vmem = pl.BlockSpec(memory_space=pltpu.VMEM)
    given = pl.BlockSpec(memory_space=pltpu.HBM) if copied else vmem
    size = sum(o.size * o.dtype.itemsize for o in operands)
    scratch = [pltpu.VMEM(o.shape, o.dtype) for o in operands[1:]]
    return pl.pallas_call(
        kernel,
        out_shape=out_shape,
        in_specs=[pl.BlockSpec(memory_space=pltpu.SMEM)] + [given] * (len(operands) - 1),
        out_specs=jax.tree.map(lambda _: vmem, out_shape),
        scratch_shapes=scratch + [pltpu.SemaphoreType.DMA((16,))] if copied else [],
        compiler_params=pltpu.CompilerParams(vmem_limit_bytes=(60 if copied else 40) * 1024 * 1024),
        cost_estimate=pl.CostEstimate(flops=flops, bytes_accessed=size, transcendentals=0),
    )(*operands)


def per_device(tokens, norm_gain, w_inner, w_outer):
    at = coordinates()
    zt = at["zt"]
    rows, cols = tokens.shape
    d_dev, f_dev = w_inner.shape
    half = f_dev // 2
    place = jnp.stack([at[a] for a in ("x", "zq", "y", "zh", "c", "zt")]).astype(jnp.int32)

    def weight_half(which, axis, array):
        return lax.dynamic_slice_in_dim(array, which * half, half, axis)

    both = jnp.concatenate([tokens, jnp.broadcast_to(norm_gain[None], (GAIN_ROWS, cols))], axis=0)
    swapped = swap_halves(weight_half(zt, 1, w_inner), weight_half(1 - zt, 1, w_inner))
    z1, z2 = (send(both, ("zt", "zh"), k) for k in (1, 2))
    z3 = send(after(both, *swapped), ("zt", "zh"), 3)
    own, swap_cross = swap_blocks(w_outer)
    both = jnp.stack([both, z1, z2, z3])

    inner = after(jnp.stack(swapped), both, own)
    inner = jnp.stack([inner] + [send(inner, ("zq",), k) for k in (1, 2, 3)], axis=1)
    cross = swap_cross(after(w_outer, both, own))
    y1 = send(after(both, own), ("y",), 1)

    in1, in3 = from_neighbours(after(inner, y1, cross), "x")
    outer = spread_blocks(after(jnp.stack([own, cross]), inner, y1), at)

    in2a, in2b = from_far(after(in1, outer), after(in3, outer), "x", 1)
    out1, out3 = from_neighbours(after(outer, in1, in3), "x")
    y3 = send(after(both, outer), ("y",), 3)
    y2 = send(after(both, in2a, in2b), ("y",), 2)

    both = jnp.stack([both, y1, y2, y3])
    other = send(after(both, out1, out3), ("c",), 1)
    out2a, out2b = from_far(after(out1, y2, y3), after(out3, y2, y3), "x", 1)

    flops = 2 * 2 * rows * half * 16 * cols
    act = call(
        hidden_kernel,
        jax.ShapeDtypeStruct((2, rows, half), jnp.bfloat16),
        flops, place, both, other, inner, in1, in2a[0], in2b[0], in3, copied=True,
    )
    act_other = send(act, ("c",), 1)
    shape = jax.ShapeDtypeStruct((4, 2, rows, cols), jnp.bfloat16)
    parts = []
    for a in (0, 1):
        sent = call(
            functools.partial(out_kernel, a), shape, flops // 2,
            place, act, act_other, outer, out1, out2a[0], out2b[0], out3,
        )
        total = sent[0].astype(jnp.float32) + sum(
            send(sent[k], ("y",), k).astype(jnp.float32) for k in (1, 2, 3)
        )
        parts.append((total, total.astype(jnp.bfloat16)))
    (total, stay), (_, away) = parts
    total = total[0] + sum(
        send(piece, ("zt", "zh"), k).astype(jnp.float32)
        for k, piece in ((2, away[0]), (3, away[1]), (1, stay[1]))
    )
    return total.astype(jnp.bfloat16)


def solution(mesh):
    fine = Mesh(np.asarray(mesh.devices).reshape(SIZES), AXES)
    dp, mp = ("x", "zt", "zq"), ("y", "zh", "c")
    in_specs = (P(dp, mp), P(mp), P(dp, mp), P(mp, dp))
    return jax.shard_map(
        per_device, mesh=fine, in_specs=in_specs, out_specs=P(dp, mp), check_vma=False
    )
```

```python
import functools

import jax
import jax.numpy as jnp
import numpy as np
from jax import lax
from jax.experimental import pallas as pl
from jax.experimental.pallas import tpu as pltpu
from jax.sharding import Mesh, PartitionSpec as P

epsilon = 1e-06
AXES = ("x", "zt", "zq", "y", "zh", "c")
SIZES = (4, 2, 4, 4, 2, 2)
SIZE = dict(zip(AXES, SIZES))
GAIN_ROWS = 16


def gelu_exact(values):
    return 0.5 * values * (1.0 + lax.erf(values * 0.7071067811865476))


def send(value, axes, k):
    count = int(np.prod([SIZE[a] for a in axes]))
    return lax.ppermute(value, axes, [(i, i ^ k) for i in range(count)])


def after(value, *others):
    return lax.optimization_barrier((value, *others))[0]


def swap_halves(first, second):
    both = [(a, b) for a in (0, 1) for b in (0, 1)]
    straight = lax.ppermute(first, ("zt", "c"), [(2 * a + b, 2 * b + a) for a, b in both])
    crossed = lax.ppermute(second, ("zt", "c"), [(2 * a + b, 2 * b + 1 - a) for a, b in both])
    return straight, crossed


def from_neighbours(value, axis):
    return [send(value, (axis,), k) for k in (1, 3)]


def from_far(one, three, axis, split):
    return send(three[:split], (axis,), 1), send(one[split:], (axis,), 3)


def swap_blocks(block):
    place = [(a, q) for a in range(2) for q in range(4)]
    axes = ("zt", "zq", "c")
    own = [(8 * a + 2 * q + a, 8 * a + 2 * q + q // 2) for a, q in place]
    own += [(8 * a + 2 * q + 1 - a, 8 * a + 2 * q + 1 - q // 2) for a, q in place]
    cross = [(8 * a + 2 * q + 1 - a, 8 * (1 - a) + 2 * q + q // 2) for a, q in place]
    cross += [(8 * a + 2 * q + a, 8 * a + 2 * q + 1 - q // 2) for a, q in place]
    return lax.ppermute(block, axes, own), lax.ppermute(block, axes, cross)


def spread_blocks(blocks, at):
    got = []
    for k in (1, 2, 3):
        pairs = [(2 * q + q // 2, 2 * (q ^ k) + q // 2) for q in range(4)]
        pairs += [(2 * q + 1 - q // 2, 2 * q + (q // 2 + (k == 1)) % 2) for q in range(4)]
        got.append(lax.ppermute(blocks, ("zq", "c"), pairs))
    one, two, three = got
    here = at["zq"] // 2 == at["c"]
    return jnp.stack([jnp.where(here, blocks, two), jnp.where(here, one, three)], axis=1)


def coordinates():
    return {a: lax.axis_index(a) for a in AXES}


def hidden_kernel(place, *refs):
    far, act, held, sems = refs[:7], refs[7], refs[8:15], refs[15]
    x, zq, y, zh, c = (place[i] for i in range(5))
    copies = []
    for i in range(far[0].shape[0]):
        for ref, near in zip(far[:2], held[:2]):
            copies.append(pltpu.make_async_copy(ref.at[i], near.at[i], sems.at[len(copies)]))
    for ref, near in zip(far[2:], held[2:]):
        copies.append(pltpu.make_async_copy(ref, near, sems.at[len(copies)]))
    for copy in copies:
        copy.start()
    mine, other, w0, w1, w2a, w2b, w3 = held
    cores = (mine, other)
    rows = act.shape[1]
    width = mine.shape[3]
    count = 2 * mine.shape[0] * 2 * width
    slots = [[w.at[s] for s in range(2)] for w in (w0, w1)] + [[w2a, w2b]] + [[w3.at[s] for s in range(2)]]
    for copy in copies[:8]:
        copy.wait()
    norms = []
    for a in range(2):
        blocks = [(ref, i, 2 * a + j) for i in range(4) for ref in cores for j in range(2)]
        total = jnp.zeros((rows, width), jnp.float32)
        for ref, i, j in blocks:
            total += ref[i, j, :rows, :].astype(jnp.float32)
        center = jnp.sum(total, axis=1, keepdims=True) * (1.0 / count)
        total = jnp.zeros((rows, width), jnp.float32)
        for ref, i, j in blocks:
            total += jnp.square(ref[i, j, :rows, :].astype(jnp.float32) - center)
        spread = jnp.sum(total, axis=1, keepdims=True) * (1.0 / count)
        norms.append((center, lax.rsqrt(spread + epsilon)))
    for copy in copies[8:]:
        copy.wait()
    for a, (center, scale) in enumerate(norms):
        acc = jnp.zeros((rows, act.shape[2]), jnp.float32)
        for k in range(4):
            i = x ^ k ^ y
            for s in range(2):
                weights = slots[k][s]
                j = 2 * a + (zh ^ c ^ s)
                for ck, ref in enumerate(cores):
                    first = 2 * (c ^ ck)
                    block = jnp.concatenate(
                        [weights[first ^ zq], weights[(first + 1) ^ zq]], axis=0
                    )
                    gain = ref[i, j, rows : rows + GAIN_ROWS, :].astype(jnp.float32)[0:1]
                    values = ref[i, j, :rows, :].astype(jnp.float32)
                    normed = ((values - center) * scale * gain).astype(jnp.bfloat16)
                    acc += jnp.dot(normed, block, preferred_element_type=jnp.float32)
        act[a] = gelu_exact(acc).astype(act.dtype)


def out_kernel(a, place, act, act_other, w0, w1, w2a, w2b, w3, out):
    x, zq, y, zh, c, zt = (place[i] for i in range(6))
    half = act.shape[2]
    slots = [[w.at[s] for s in range(2)] for w in (w0, w1)] + [[w2a, w2b]] + [[w3.at[s] for s in range(2)]]
    for k in range(4):
        for s in range(2):
            total = None
            for core, part in ((c, act), (1 - c, act_other)):
                units = pl.ds(pl.multiple_of(core * half, half), half)
                block = jnp.concatenate(
                    [slots[k][s][zq & 1, units, :], slots[k][s][1 - (zq & 1), units, :]], axis=1
                )
                term = jnp.dot(part[a], block, preferred_element_type=jnp.float32)
                total = term if total is None else total + term
            out[x ^ k ^ y, zh ^ zt ^ s] = total.astype(out.dtype)


def call(kernel, out_shape, flops, *operands, copied=False):
    vmem = pl.BlockSpec(memory_space=pltpu.VMEM)
    given = pl.BlockSpec(memory_space=pltpu.HBM) if copied else vmem
    size = sum(o.size * o.dtype.itemsize for o in operands)
    scratch = [pltpu.VMEM(o.shape, o.dtype) for o in operands[1:]]
    return pl.pallas_call(
        kernel,
        out_shape=out_shape,
        in_specs=[pl.BlockSpec(memory_space=pltpu.SMEM)] + [given] * (len(operands) - 1),
        out_specs=jax.tree.map(lambda _: vmem, out_shape),
        scratch_shapes=scratch + [pltpu.SemaphoreType.DMA((16,))] if copied else [],
        compiler_params=pltpu.CompilerParams(vmem_limit_bytes=(60 if copied else 40) * 1024 * 1024),
        cost_estimate=pl.CostEstimate(flops=flops, bytes_accessed=size, transcendentals=0),
    )(*operands)


def per_device(tokens, norm_gain, w_inner, w_outer):
    at = coordinates()
    zt = at["zt"]
    rows, cols = tokens.shape
    d_dev, f_dev = w_inner.shape
    half = f_dev // 2
    place = jnp.stack([at[a] for a in ("x", "zq", "y", "zh", "c", "zt")]).astype(jnp.int32)

    def weight_half(which, axis, array):
        return lax.dynamic_slice_in_dim(array, which * half, half, axis)

    both = jnp.concatenate([tokens, jnp.broadcast_to(norm_gain[None], (GAIN_ROWS, cols))], axis=0)
    z3, z2, z1 = (send(both, ("zt", "zh"), k) for k in (3, 2, 1))
    swapped = swap_halves(weight_half(zt, 1, w_inner), weight_half(1 - zt, 1, w_inner))
    own, cross = swap_blocks(after(w_outer, *swapped))
    both = jnp.stack([both, z1, z2, z3])

    inner = after(jnp.stack(swapped), both, own, cross)
    inner = jnp.stack([inner] + [send(inner, ("zq",), k) for k in (1, 2, 3)], axis=1)
    y1, y3 = from_neighbours(after(both, own, cross), "y")

    in1, in3 = from_neighbours(after(inner, y1, y3), "x")
    outer = spread_blocks(after(jnp.stack([own, cross]), inner, y1, y3), at)

    in2a, in2b = from_far(after(in1, outer), after(in3, outer), "x", 1)
    out1, out3 = from_neighbours(after(outer, in1, in3), "x")
    y2 = send(after(both, outer), ("y",), 2)

    both = jnp.stack([both, y1, y2, y3])
    other = send(after(both, out1, out3, in2a, in2b), ("c",), 1)
    out2a, out2b = from_far(after(out1, y2), after(out3, y2), "x", 1)

    flops = 2 * 2 * rows * half * 16 * cols
    act = call(
        hidden_kernel,
        jax.ShapeDtypeStruct((2, rows, half), jnp.bfloat16),
        flops, place, both, other, inner, in1, in2a[0], in2b[0], in3, copied=True,
    )
    act_other = send(act, ("c",), 1)
    shape = jax.ShapeDtypeStruct((4, 2, rows, cols), jnp.bfloat16)
    parts = []
    for a in (0, 1):
        sent = call(
            functools.partial(out_kernel, a), shape, flops // 2,
            place, act, act_other, outer, out1, out2a[0], out2b[0], out3,
        )
        total = sent[0].astype(jnp.float32) + sum(
            send(sent[k], ("y",), k).astype(jnp.float32) for k in (1, 2, 3)
        )
        parts.append((total, total.astype(jnp.bfloat16)))
    (total, stay), (_, away) = parts
    total = total[0] + sum(
        send(piece, ("zt", "zh"), k).astype(jnp.float32)
        for k, piece in ((2, away[0]), (3, away[1]), (1, stay[1]))
    )
    return total.astype(jnp.bfloat16)


def solution(mesh):
    fine = Mesh(np.asarray(mesh.devices).reshape(SIZES), AXES)
    dp, mp = ("x", "zt", "zq"), ("y", "zh", "c")
    in_specs = (P(dp, mp), P(mp), P(dp, mp), P(mp, dp))
    return jax.shard_map(
        per_device, mesh=fine, in_specs=in_specs, out_specs=P(dp, mp), check_vma=False
    )
```

```python
import functools

import jax
import jax.numpy as jnp
import numpy as np
from jax import lax
from jax.experimental import pallas as pl
from jax.experimental.pallas import tpu as pltpu
from jax.sharding import Mesh, PartitionSpec as P

epsilon = 1e-06
AXES = ("x", "zt", "zq", "y", "zh", "c")
SIZES = (4, 2, 4, 4, 2, 2)
SIZE = dict(zip(AXES, SIZES))
GAIN_ROWS = 16


def gelu_exact(values):
    return 0.5 * values * (1.0 + lax.erf(values * 0.7071067811865476))


def send(value, axes, k):
    count = int(np.prod([SIZE[a] for a in axes]))
    return lax.ppermute(value, axes, [(i, i ^ k) for i in range(count)])


def after(value, *others):
    return lax.optimization_barrier((value, *others))[0]


def swap_halves(first, second):
    both = [(a, b) for a in (0, 1) for b in (0, 1)]
    straight = lax.ppermute(first, ("zt", "c"), [(2 * a + b, 2 * b + a) for a, b in both])
    crossed = lax.ppermute(second, ("zt", "c"), [(2 * a + b, 2 * b + 1 - a) for a, b in both])
    return straight, crossed


def from_neighbours(value, axis):
    return [send(value, (axis,), k) for k in (1, 3)]


def from_far(one, three, axis, split):
    return send(three[:split], (axis,), 1), send(one[split:], (axis,), 3)


def swap_blocks(block):
    place = [(a, q) for a in range(2) for q in range(4)]
    axes = ("zt", "zq", "c")
    own = [(8 * a + 2 * q + a, 8 * a + 2 * q + q // 2) for a, q in place]
    own += [(8 * a + 2 * q + 1 - a, 8 * a + 2 * q + 1 - q // 2) for a, q in place]
    cross = [(8 * a + 2 * q + 1 - a, 8 * (1 - a) + 2 * q + q // 2) for a, q in place]
    cross += [(8 * a + 2 * q + a, 8 * a + 2 * q + 1 - q // 2) for a, q in place]
    return lax.ppermute(block, axes, own), lax.ppermute(block, axes, cross)


def spread_blocks(blocks, at):
    got = []
    for k in (1, 2, 3):
        pairs = [(2 * q + q // 2, 2 * (q ^ k) + q // 2) for q in range(4)]
        pairs += [(2 * q + 1 - q // 2, 2 * q + (q // 2 + (k == 1)) % 2) for q in range(4)]
        got.append(lax.ppermute(blocks, ("zq", "c"), pairs))
    one, two, three = got
    here = at["zq"] // 2 == at["c"]
    return jnp.stack([jnp.where(here, blocks, two), jnp.where(here, one, three)], axis=1)


def coordinates():
    return {a: lax.axis_index(a) for a in AXES}


def hidden_kernel(place, *refs):
    far, act, held, sems = refs[:7], refs[7], refs[8:15], refs[15]
    x, zq, y, zh, c = (place[i] for i in range(5))
    copies = []
    for i in range(far[0].shape[0]):
        for ref, near in zip(far[:2], held[:2]):
            copies.append(pltpu.make_async_copy(ref.at[i], near.at[i], sems.at[len(copies)]))
    for ref, near in zip(far[2:], held[2:]):
        copies.append(pltpu.make_async_copy(ref, near, sems.at[len(copies)]))
    for copy in copies:
        copy.start()
    mine, other, w0, w1, w2a, w2b, w3 = held
    cores = (mine, other)
    rows = act.shape[1]
    width = mine.shape[3]
    count = 2 * mine.shape[0] * 2 * width
    slots = [[w.at[s] for s in range(2)] for w in (w0, w1)] + [[w2a, w2b]] + [[w3.at[s] for s in range(2)]]
    for copy in copies[:8]:
        copy.wait()
    norms = []
    for a in range(2):
        blocks = [(ref, i, 2 * a + j) for i in range(4) for ref in cores for j in range(2)]
        total = jnp.zeros((rows, width), jnp.float32)
        for ref, i, j in blocks:
            total += ref[i, j, :rows, :].astype(jnp.float32)
        center = jnp.sum(total, axis=1, keepdims=True) * (1.0 / count)
        total = jnp.zeros((rows, width), jnp.float32)
        for ref, i, j in blocks:
            total += jnp.square(ref[i, j, :rows, :].astype(jnp.float32) - center)
        spread = jnp.sum(total, axis=1, keepdims=True) * (1.0 / count)
        norms.append((center, lax.rsqrt(spread + epsilon)))
    for copy in copies[8:]:
        copy.wait()
    for a, (center, scale) in enumerate(norms):
        acc = jnp.zeros((rows, act.shape[2]), jnp.float32)
        for k in range(4):
            i = x ^ k ^ y
            for s in range(2):
                weights = slots[k][s]
                j = 2 * a + (zh ^ c ^ s)
                for ck, ref in enumerate(cores):
                    first = 2 * (c ^ ck)
                    block = jnp.concatenate(
                        [weights[first ^ zq], weights[(first + 1) ^ zq]], axis=0
                    )
                    gain = ref[i, j, rows : rows + GAIN_ROWS, :].astype(jnp.float32)[0:1]
                    values = ref[i, j, :rows, :].astype(jnp.float32)
                    normed = ((values - center) * scale * gain).astype(jnp.bfloat16)
                    acc += jnp.dot(normed, block, preferred_element_type=jnp.float32)
        act[a] = gelu_exact(acc).astype(act.dtype)


def out_kernel(a, place, act, act_other, w0, w1, w2a, w2b, w3, out):
    x, zq, y, zh, c, zt = (place[i] for i in range(6))
    half = act.shape[2]
    slots = [[w.at[s] for s in range(2)] for w in (w0, w1)] + [[w2a, w2b]] + [[w3.at[s] for s in range(2)]]
    for k in range(4):
        for s in range(2):
            total = None
            for core, part in ((c, act), (1 - c, act_other)):
                units = pl.ds(pl.multiple_of(core * half, half), half)
                block = jnp.concatenate(
                    [slots[k][s][zq & 1, units, :], slots[k][s][1 - (zq & 1), units, :]], axis=1
                )
                term = jnp.dot(part[a], block, preferred_element_type=jnp.float32)
                total = term if total is None else total + term
            out[x ^ k ^ y, zh ^ zt ^ s] = total.astype(out.dtype)


def call(kernel, out_shape, flops, *operands, copied=False):
    vmem = pl.BlockSpec(memory_space=pltpu.VMEM)
    given = pl.BlockSpec(memory_space=pltpu.HBM) if copied else vmem
    size = sum(o.size * o.dtype.itemsize for o in operands)
    scratch = [pltpu.VMEM(o.shape, o.dtype) for o in operands[1:]]
    return pl.pallas_call(
        kernel,
        out_shape=out_shape,
        in_specs=[pl.BlockSpec(memory_space=pltpu.SMEM)] + [given] * (len(operands) - 1),
        out_specs=jax.tree.map(lambda _: vmem, out_shape),
        scratch_shapes=scratch + [pltpu.SemaphoreType.DMA((16,))] if copied else [],
        compiler_params=pltpu.CompilerParams(vmem_limit_bytes=(60 if copied else 40) * 1024 * 1024),
        cost_estimate=pl.CostEstimate(flops=flops, bytes_accessed=size, transcendentals=0),
    )(*operands)


def per_device(tokens, norm_gain, w_inner, w_outer):
    at = coordinates()
    zt = at["zt"]
    rows, cols = tokens.shape
    d_dev, f_dev = w_inner.shape
    half = f_dev // 2
    place = jnp.stack([at[a] for a in ("x", "zq", "y", "zh", "c", "zt")]).astype(jnp.int32)

    def weight_half(which, axis, array):
        return lax.dynamic_slice_in_dim(array, which * half, half, axis)

    both = jnp.concatenate([tokens, jnp.broadcast_to(norm_gain[None], (GAIN_ROWS, cols))], axis=0)
    z3, z2, z1 = (send(both, ("zt", "zh"), k) for k in (3, 2, 1))
    swapped = swap_halves(weight_half(zt, 1, w_inner), weight_half(1 - zt, 1, w_inner))
    own, cross = swap_blocks(after(w_outer, *swapped))
    both = jnp.stack([both, z1, z2, z3])

    inner = after(jnp.stack(swapped), both, own, cross)
    inner = jnp.stack([inner] + [send(inner, ("zq",), k) for k in (1, 2, 3)], axis=1)
    y1, y3 = from_neighbours(after(both, own, cross), "y")

    in1, in3 = from_neighbours(after(inner, y1, y3), "x")
    outer = spread_blocks(after(jnp.stack([own, cross]), inner, y1, y3), at)

    in2a, in2b = from_far(after(in1, outer), after(in3, outer), "x", 1)
    out1, out3 = from_neighbours(after(outer, in1, in3), "x")
    y2 = send(after(both, in2a, in2b), ("y",), 2)

    both = jnp.stack([both, y1, y2, y3])
    other = send(after(both, out1, out3), ("c",), 1)
    out2a, out2b = from_far(after(out1, y2), after(out3, y2), "x", 1)

    flops = 2 * 2 * rows * half * 16 * cols
    act = call(
        hidden_kernel,
        jax.ShapeDtypeStruct((2, rows, half), jnp.bfloat16),
        flops, place, both, other, inner, in1, in2a[0], in2b[0], in3, copied=True,
    )
    act_other = send(act, ("c",), 1)
    shape = jax.ShapeDtypeStruct((4, 2, rows, cols), jnp.bfloat16)
    parts = []
    for a in (0, 1):
        sent = call(
            functools.partial(out_kernel, a), shape, flops // 2,
            place, act, act_other, outer, out1, out2a[0], out2b[0], out3,
        )
        total = sent[0].astype(jnp.float32) + sum(
            send(sent[k], ("y",), k).astype(jnp.float32) for k in (1, 2, 3)
        )
        parts.append((total, total.astype(jnp.bfloat16)))
    (total, stay), (_, away) = parts
    total = total[0] + sum(
        send(piece, ("zt", "zh"), k).astype(jnp.float32)
        for k, piece in ((2, away[0]), (3, away[1]), (1, stay[1]))
    )
    return total.astype(jnp.bfloat16)


def solution(mesh):
    fine = Mesh(np.asarray(mesh.devices).reshape(SIZES), AXES)
    dp, mp = ("x", "zt", "zq"), ("y", "zh", "c")
    in_specs = (P(dp, mp), P(mp), P(dp, mp), P(mp, dp))
    return jax.shard_map(
        per_device, mesh=fine, in_specs=in_specs, out_specs=P(dp, mp), check_vma=False
    )
```

```python
import functools

import jax
import jax.numpy as jnp
import numpy as np
from jax import lax
from jax.experimental import pallas as pl
from jax.experimental.pallas import tpu as pltpu
from jax.sharding import Mesh, PartitionSpec as P

epsilon = 1e-06
AXES = ("x", "zt", "zq", "y", "zh", "c")
SIZES = (4, 2, 4, 4, 2, 2)
SIZE = dict(zip(AXES, SIZES))
GAIN_ROWS = 16


def gelu_exact(values):
    return 0.5 * values * (1.0 + lax.erf(values * 0.7071067811865476))


def send(value, axes, k):
    count = int(np.prod([SIZE[a] for a in axes]))
    return lax.ppermute(value, axes, [(i, i ^ k) for i in range(count)])


def after(value, *others):
    return lax.optimization_barrier((value, *others))[0]


def swap_halves(first, second):
    both = [(a, b) for a in (0, 1) for b in (0, 1)]
    straight = lax.ppermute(first, ("zt", "c"), [(2 * a + b, 2 * b + a) for a, b in both])
    crossed = lax.ppermute(second, ("zt", "c"), [(2 * a + b, 2 * b + 1 - a) for a, b in both])
    return straight, crossed


def from_neighbours(value, axis):
    return [send(value, (axis,), k) for k in (1, 3)]


def from_far(one, three, axis, split):
    return send(three[:split], (axis,), 1), send(one[split:], (axis,), 3)


def swap_blocks(block):
    place = [(a, q) for a in range(2) for q in range(4)]
    axes = ("zt", "zq", "c")
    own = [(8 * a + 2 * q + a, 8 * a + 2 * q + q // 2) for a, q in place]
    own += [(8 * a + 2 * q + 1 - a, 8 * a + 2 * q + 1 - q // 2) for a, q in place]
    cross = [(8 * a + 2 * q + 1 - a, 8 * (1 - a) + 2 * q + q // 2) for a, q in place]
    cross += [(8 * a + 2 * q + a, 8 * a + 2 * q + 1 - q // 2) for a, q in place]
    return lax.ppermute(block, axes, own), lax.ppermute(block, axes, cross)


def spread_blocks(blocks, at):
    got = []
    for k in (1, 2, 3):
        pairs = [(2 * q + q // 2, 2 * (q ^ k) + q // 2) for q in range(4)]
        pairs += [(2 * q + 1 - q // 2, 2 * q + (q // 2 + (k == 1)) % 2) for q in range(4)]
        got.append(lax.ppermute(blocks, ("zq", "c"), pairs))
    one, two, three = got
    here = at["zq"] // 2 == at["c"]
    return jnp.stack([jnp.where(here, blocks, two), jnp.where(here, one, three)], axis=1)


def coordinates():
    return {a: lax.axis_index(a) for a in AXES}


def hidden_kernel(place, *refs):
    far, act, held, sems = refs[:7], refs[7], refs[8:15], refs[15]
    x, zq, y, zh, c = (place[i] for i in range(5))
    copies = []
    for i in range(far[0].shape[0]):
        for ref, near in zip(far[:2], held[:2]):
            copies.append(pltpu.make_async_copy(ref.at[i], near.at[i], sems.at[len(copies)]))
    for ref, near in zip(far[2:], held[2:]):
        copies.append(pltpu.make_async_copy(ref, near, sems.at[len(copies)]))
    for copy in copies:
        copy.start()
    mine, other, w0, w1, w2a, w2b, w3 = held
    cores = (mine, other)
    rows = act.shape[1]
    width = mine.shape[3]
    count = 2 * mine.shape[0] * 2 * width
    slots = [[w.at[s] for s in range(2)] for w in (w0, w1)] + [[w2a, w2b]] + [[w3.at[s] for s in range(2)]]
    for copy in copies[:8]:
        copy.wait()
    norms = []
    for a in range(2):
        blocks = [(ref, i, 2 * a + j) for i in range(4) for ref in cores for j in range(2)]
        total = jnp.zeros((rows, width), jnp.float32)
        for ref, i, j in blocks:
            total += ref[i, j, :rows, :].astype(jnp.float32)
        center = jnp.sum(total, axis=1, keepdims=True) * (1.0 / count)
        total = jnp.zeros((rows, width), jnp.float32)
        for ref, i, j in blocks:
            total += jnp.square(ref[i, j, :rows, :].astype(jnp.float32) - center)
        spread = jnp.sum(total, axis=1, keepdims=True) * (1.0 / count)
        norms.append((center, lax.rsqrt(spread + epsilon)))
    for copy in copies[8:]:
        copy.wait()
    for a, (center, scale) in enumerate(norms):
        acc = jnp.zeros((rows, act.shape[2]), jnp.float32)
        for k in range(4):
            i = x ^ k ^ y
            for s in range(2):
                weights = slots[k][s]
                j = 2 * a + (zh ^ c ^ s)
                for ck, ref in enumerate(cores):
                    first = 2 * (c ^ ck)
                    block = jnp.concatenate(
                        [weights[first ^ zq], weights[(first + 1) ^ zq]], axis=0
                    )
                    gain = ref[i, j, rows : rows + GAIN_ROWS, :].astype(jnp.float32)[0:1]
                    values = ref[i, j, :rows, :].astype(jnp.float32)
                    normed = ((values - center) * scale * gain).astype(jnp.bfloat16)
                    acc += jnp.dot(normed, block, preferred_element_type=jnp.float32)
        act[a] = gelu_exact(acc).astype(act.dtype)


def out_kernel(a, place, act, act_other, w0, w1, w2a, w2b, w3, out):
    x, zq, y, zh, c, zt = (place[i] for i in range(6))
    half = act.shape[2]
    slots = [[w.at[s] for s in range(2)] for w in (w0, w1)] + [[w2a, w2b]] + [[w3.at[s] for s in range(2)]]
    for k in range(4):
        for s in range(2):
            total = None
            for core, part in ((c, act), (1 - c, act_other)):
                units = pl.ds(pl.multiple_of(core * half, half), half)
                block = jnp.concatenate(
                    [slots[k][s][zq & 1, units, :], slots[k][s][1 - (zq & 1), units, :]], axis=1
                )
                term = jnp.dot(part[a], block, preferred_element_type=jnp.float32)
                total = term if total is None else total + term
            out[x ^ k ^ y, zh ^ zt ^ s] = total.astype(out.dtype)


def call(kernel, out_shape, flops, *operands, copied=False):
    vmem = pl.BlockSpec(memory_space=pltpu.VMEM)
    given = pl.BlockSpec(memory_space=pltpu.HBM) if copied else vmem
    size = sum(o.size * o.dtype.itemsize for o in operands)
    scratch = [pltpu.VMEM(o.shape, o.dtype) for o in operands[1:]]
    return pl.pallas_call(
        kernel,
        out_shape=out_shape,
        in_specs=[pl.BlockSpec(memory_space=pltpu.SMEM)] + [given] * (len(operands) - 1),
        out_specs=jax.tree.map(lambda _: vmem, out_shape),
        scratch_shapes=scratch + [pltpu.SemaphoreType.DMA((16,))] if copied else [],
        compiler_params=pltpu.CompilerParams(vmem_limit_bytes=(60 if copied else 40) * 1024 * 1024),
        cost_estimate=pl.CostEstimate(flops=flops, bytes_accessed=size, transcendentals=0),
    )(*operands)


def per_device(tokens, norm_gain, w_inner, w_outer):
    at = coordinates()
    zt = at["zt"]
    rows, cols = tokens.shape
    d_dev, f_dev = w_inner.shape
    half = f_dev // 2
    place = jnp.stack([at[a] for a in ("x", "zq", "y", "zh", "c", "zt")]).astype(jnp.int32)

    def weight_half(which, axis, array):
        return lax.dynamic_slice_in_dim(array, which * half, half, axis)

    both = jnp.concatenate([tokens, jnp.broadcast_to(norm_gain[None], (GAIN_ROWS, cols))], axis=0)
    z3, z2, z1 = (send(both, ("zt", "zh"), k) for k in (3, 2, 1))
    swapped = swap_halves(weight_half(zt, 1, w_inner), weight_half(1 - zt, 1, w_inner))
    own, cross = swap_blocks(after(w_outer, *swapped))
    both = jnp.stack([both, z1, z2, z3])

    inner = after(jnp.stack(swapped), both, own, cross)
    inner = jnp.stack([inner] + [send(inner, ("zq",), k) for k in (1, 2, 3)], axis=1)
    y1, y3 = from_neighbours(after(both, own, cross), "y")

    in1, in3 = from_neighbours(after(inner, y1, y3), "x")
    outer = spread_blocks(after(jnp.stack([own, cross]), inner, y1, y3), at)

    in2a, in2b = from_far(after(in1, outer), after(in3, outer), "x", 1)
    out1, out3 = from_neighbours(after(outer, in1, in3), "x")
    y2 = send(after(both, in2a, in2b), ("y",), 2)

    both = jnp.stack([both, y1, y2, y3])
    other = send(after(both, out1, out3), ("c",), 1)
    out2a, out2b = from_far(after(out1, y2), after(out3, y2), "x", 1)

    flops = 2 * 2 * rows * half * 16 * cols
    act = call(
        hidden_kernel,
        jax.ShapeDtypeStruct((2, rows, half), jnp.bfloat16),
        flops, place, both, other, inner, in1, in2a[0], in2b[0], in3, copied=True,
    )
    act_other = send(act, ("c",), 1)
    shape = jax.ShapeDtypeStruct((4, 2, rows, cols), jnp.bfloat16)
    parts = []
    for a in (0, 1):
        sent = call(
            functools.partial(out_kernel, a), shape, flops // 2,
            place, act, act_other, outer, out1, out2a[0], out2b[0], out3,
        )
        total = sent[0].astype(jnp.float32) + sum(
            send(sent[k], ("y",), k).astype(jnp.float32) for k in (1, 2, 3)
        )
        parts.append((total, total.astype(jnp.bfloat16)))
    (total, stay), (_, away) = parts
    total = total[0] + sum(
        send(piece, ("zt", "zh"), k).astype(jnp.float32)
        for k, piece in ((1, stay[1]), (3, away[1]), (2, away[0]))
    )
    return total.astype(jnp.bfloat16)


def solution(mesh):
    fine = Mesh(np.asarray(mesh.devices).reshape(SIZES), AXES)
    dp, mp = ("x", "zt", "zq"), ("y", "zh", "c")
    in_specs = (P(dp, mp), P(mp), P(dp, mp), P(mp, dp))
    return jax.shard_map(
        per_device, mesh=fine, in_specs=in_specs, out_specs=P(dp, mp), check_vma=False
    )
```
